128 devices in a mesh: leaf: 64 (over x, y, z), rhs: 2 (over core).
Axes of the slice: x: 4, y: 4, z: 4, core: 2. Of those that a mesh axis runs over, the one named last changes fastest.
Arguments:
- points: bfloat16 [8192, 8, 256], P('leaf'), may hold values from -5 to 5
- values: bfloat16 [8192, 16, 256], P('leaf', 'rhs'), parts along dimension 1, may hold values from -6 to 6
- counts: int32 [8192], P('leaf'), may hold values from 128 to 256
- leaf_basis: bfloat16 [8192, 64, 256], P('leaf'), may hold values from -0.375 to 0.375
- transfer: bfloat16 [8192, 64, 64], P('leaf'), may hold values from -0.5 to 0.5
- leaf_skeleton: bfloat16 [8192, 8, 64], P('leaf'), may hold values from -5 to 5
- upper_skeleton: bfloat16 [4096, 8, 64], P('leaf'), may hold values from -5 to 5
- near_list: int32 [8192, 6], P('leaf'), may hold values from 0 to 8191, as said below
- far_owner: int32 [8192, 8], P('leaf'), may hold values from 0 to 63, all different within a row; in each aligned block of 128 rows (0 to 127, 128 to 255, ...) at most 32 rows name the same one
- far_local: int32 [8192, 8], P('leaf'), may hold values from 0 to 127
- upper_owner: int32 [4096, 8], P('leaf'), may hold values from 0 to 63, all different within a row; in each aligned block of 64 rows (0 to 63, 64 to 127, ...) at most 16 rows name the same one
- upper_local: int32 [4096, 8], P('leaf'), may hold values from 0 to 63
Outputs:
- product: float32 [8192, 16, 256], P('leaf', 'rhs'), parts along dimension 1
The draws below stay inside these ranges and needn't reach their ends.
There are 2 independent parts, one for each index of `rhs`. The reference program is written for one: setup_inputs(seed, part) draws one part's arguments, and reference() takes and returns one part's arrays. A program takes and returns all parts, laid end to end along the dimension named above; an argument that names none is the same for every part. Nothing has to cross between parts.
Inputs may be any that keep to these rules, and one draw needn't show every extreme that they name: `near_list`: entry 0 of leaf l's list is l itself; every entry lies within 4 leaves of the block of 128 leaves that holds l, and some lists reach both ends of that range where the grid of leaves allows. `far_owner`: A row's 8 owners are different; among the rows of one device (aligned blocks of 128 rows) no owner is named by more than 32 entries, and some owner by exactly that many. `upper_owner`: A row's 8 owners are different; among the rows of one device (aligned blocks of 64 rows) no owner is named by more than 16 entries, and some owner by exactly that many.
All inputs are finite; a program needn't handle non-finite values.
Results may differ from the reference program's by a relative error of at most 0.0032.
Values may be sent and summed in bfloat16 or wider, within the bound.
No kernel may reach another device: no remote copies, remote signals or barrier semaphores. Data moves between devices by JAX's collectives and lax.ppermute only.
A program may use at most 128 MiB of HBM per device.

```python
import math
import jax
import jax.numpy as jnp
import numpy as np
from jax import lax

LEAF = 256
RANK = 64
DIM = 8
C = 8
LEAF_DEV = 128
NEAR = 6
FAR = 8
HALO = 4
OWNERS = 64
PAR_DEV = 64
LEAVES = 8192
PARENTS = 4096
CAP_LEAF = 32
CAP_UPPER = 16


def draw_near_list(key, part):
    key = jax.random.fold_in(key, 11)
    rows = jnp.arange(LEAVES, dtype=jnp.int32)
    start = rows // LEAF_DEV * LEAF_DEV
    offsets = jax.random.randint(key, (LEAVES, NEAR), -HALO, LEAF_DEV + HALO)
    picks = start[:, None] + offsets
    position = rows % LEAF_DEV
    lowest = jnp.where(position == 0, start - HALO, picks[:, 1])
    second = jnp.where(position == LEAF_DEV - 1, start + LEAF_DEV + HALO - 1, lowest)
    picks = picks.at[:, 1].set(second)
    picks = picks.at[:, 0].set(rows)
    return jnp.clip(picks, 0, LEAVES - 1).astype(jnp.int32)


def with_ends(array, stream_key, least, top_value):
    index_at = [jax.random.randint(jax.random.fold_in(stream_key, axis), (), 0, length) for axis, length in enumerate(array.shape)]
    widest = array.shape.index(max(array.shape))
    neighbour = index_at[:widest] + [(index_at[widest] + 1) % array.shape[widest]] + index_at[widest + 1:]
    return array.at[tuple(index_at)].set(least).at[tuple(neighbour)].set(top_value)


def levels(own_key, extent, split, least, largest):
    factor_of, own = 1.0, jax.random.fold_in(own_key, 6)
    for axis_at, blocks in split:
        heights = jnp.exp(jax.random.uniform(jax.random.fold_in(own, axis_at), (blocks,), jnp.float32, least / len(split), largest / len(split)))
        factor_of = factor_of * jnp.repeat(heights, extent[axis_at] // blocks).reshape([-1 if axis == axis_at else 1 for axis in range(len(extent))])
    return factor_of


def assign_block(rng, own, number, rows, number_of, top, reach, lean):
    order = jax.random.permutation(rng, number_of)
    packed, ordinary = portions_of(number_of, rows * top, reach, lean, True), portions_of(number_of, rows * top, reach, lean, False)
    places = jnp.arange(number_of)

    def named(sizes, offset_by):
        used = int((sizes > 0).sum())
        fixed = max(1, used // 4)
        passed = fixed + (places - fixed + offset_by * (used - fixed)) % max(1, number_of - fixed)
        return jnp.zeros((number_of,), jnp.int32).at[order[jnp.where(places < fixed, places, passed)]].set(jnp.asarray(sizes, jnp.int32))

    sizes = jnp.where(number % 4 == 0, named(packed, number // 4), named(ordinary, number - number // 4 - 1))
    mixed = jax.random.permutation(jax.random.fold_in(own, 3), number_of)
    source_of, receiver = mixed[0:number_of // 2 * 2:2], mixed[1:number_of // 2 * 2:2]
    slack = jnp.minimum(sizes[source_of] - 1, reach - sizes[receiver]) // 2
    slack = jnp.where((source_of == order[0]) | (receiver == order[0]) | (sizes[receiver] == 0), 0, jnp.maximum(slack, 0))
    passed = jax.random.randint(jax.random.fold_in(own, 4), (number_of // 2,), 0, 1 << 20) % (slack + 1)
    sizes = sizes.at[source_of].add(-passed).at[receiver].add(passed)
    items = jnp.searchsorted(jnp.cumsum(sizes), jnp.arange(rows * top), side="right").astype(jnp.int32)
    listing = items.reshape(top, rows).T
    listing = listing[jax.random.permutation(jax.random.fold_in(own, 1), rows)]
    offset_by = jax.random.randint(jax.random.fold_in(own, 2), (rows, 1), 0, top)
    return jnp.take_along_axis(listing, (jnp.arange(top)[None, :] + offset_by) % top, axis=1)


def portions_of(amount, total, reach, skew, full):
    weights = [(1 << 20) // math.isqrt(grade ** skew) + 1 for grade in range(1, amount + 1)]
    largest = reach if full else min(reach, max(-(-total // amount), total * weights[0] // sum(weights)))
    least = 1 if total - largest >= amount - 1 else 0
    given, rest = [largest] + [least] * (amount - 1), total - largest - least * (amount - 1)
    while rest > 0:
        candidates = [i for i in range(1, amount) if given[i] < largest] or [i for i in range(1, amount) if given[i] < reach]
        mass, left = sum([weights[i] for i in candidates]), rest
        for i in candidates:
            addition = min(reach - given[i], max(1, left * weights[i] // mass), rest)
            given[i] = given[i] + addition
            rest = rest - addition
    return np.array(given)


def normal_values(own_key, extent, scale, bound, split=(), kind=jnp.bfloat16):
    loudness = levels(own_key, extent, split, -0.22, 0.18) if split else 1.0
    array = jax.random.normal(own_key, extent, jnp.float32) * scale * loudness
    return jnp.minimum(jnp.maximum(array, -bound), bound).astype(kind)


def setup_inputs(seed: int = 0, part: int = 0) -> dict:
    streams_of = jax.random.split(jax.random.key(seed), 13)
    part_splits = jax.random.split(jax.random.fold_in(streams_of[12], part), 13)
    points = normal_values(streams_of[0], (LEAVES, DIM, LEAF), 1.0, 5.0, ((0, 64),))
    values = normal_values(part_splits[1], (LEAVES, C, LEAF), 1.0, 6.0, ((0, 64),))
    counts = with_ends(jax.random.randint(streams_of[2], (LEAVES,), LEAF // 2, LEAF + 1), jax.random.fold_in(streams_of[2], 1), LEAF // 2, LEAF).astype(jnp.int32)
    leaf_basis = normal_values(streams_of[3], (LEAVES, RANK, LEAF), LEAF ** -0.5, 0.375, ((0, 64),))
    transfer = normal_values(streams_of[4], (LEAVES, RANK, RANK), (2 * RANK) ** -0.5, 0.5, ((0, 64),))
    leaf_skeleton = normal_values(streams_of[5], (LEAVES, DIM, RANK), 1.0, 5.0, ((0, 64),))
    upper_skeleton = normal_values(streams_of[6], (PARENTS, DIM, RANK), 1.0, 5.0, ((0, 64),))
    near_list = draw_near_list(jax.random.fold_in(streams_of[12], 71), part)
    far_owner_keys = jax.random.split(jax.random.fold_in(streams_of[8], 1), LEAVES // LEAF_DEV)
    far_owner_turns = jax.random.permutation(jax.random.fold_in(streams_of[8], 3), LEAVES // LEAF_DEV)
    far_owner = jax.vmap(lambda own, number: assign_block(jax.random.fold_in(streams_of[8], 2), own, number, LEAF_DEV, OWNERS, FAR, CAP_LEAF, 2))(far_owner_keys, far_owner_turns).reshape((LEAVES, FAR))
    far_local = with_ends(jax.random.randint(streams_of[9], (LEAVES, FAR), 0, LEAF_DEV), jax.random.fold_in(streams_of[9], 1), 0, LEAF_DEV - 1).astype(jnp.int32)
    upper_owner_keys = jax.random.split(jax.random.fold_in(streams_of[10], 1), PARENTS // PAR_DEV)
    upper_owner_turns = jax.random.permutation(jax.random.fold_in(streams_of[10], 3), PARENTS // PAR_DEV)
    upper_owner = jax.vmap(lambda own, number: assign_block(jax.random.fold_in(streams_of[10], 2), own, number, PAR_DEV, OWNERS, FAR, CAP_UPPER, 2))(upper_owner_keys, upper_owner_turns).reshape((PARENTS, FAR))
    upper_local = with_ends(jax.random.randint(streams_of[11], (PARENTS, FAR), 0, PAR_DEV), jax.random.fold_in(streams_of[11], 1), 0, PAR_DEV - 1).astype(jnp.int32)
    return dict(points=points, values=values, counts=counts, leaf_basis=leaf_basis, transfer=transfer, leaf_skeleton=leaf_skeleton, upper_skeleton=upper_skeleton, near_list=near_list, far_owner=far_owner, far_local=far_local, upper_owner=upper_owner, upper_local=upper_local)


SQRT_THREE = 1.7320508075688772
LENGTH_SCALE = 1.5

def matern(targets, sources):
    square = 0.0
    for coord in range(targets.shape[-2]):
        offset = targets[..., coord, :, None] - sources[..., coord, None, :]
        square = square + offset * offset
    scaled = SQRT_THREE / LENGTH_SCALE * jnp.sqrt(square)
    return (1.0 + scaled) * jnp.exp(-scaled)

def blocked(single, arrays, group):
    count = arrays[0].shape[0]
    shaped = tuple((item.reshape((count // group, group) + item.shape[1:]) for item in arrays))
    mapped = lax.map(lambda pieces: jax.vmap(single)(*pieces), shaped)
    return mapped.reshape((count,) + mapped.shape[2:])

def far_field(skeleton, coefs, source_ids, group):

    def single(target_skel, chosen):
        kernel = matern(target_skel.astype(jnp.float32)[None], skeleton[chosen].astype(jnp.float32)).astype(jnp.bfloat16)
        return jnp.einsum('fcb,fab->ca', coefs[chosen].astype(jnp.float32), kernel.astype(jnp.float32))
    return blocked(single, (skeleton, source_ids), group)

def reference(points, values, counts, leaf_basis, transfer, leaf_skeleton, upper_skeleton, near_list, far_owner, far_local, upper_owner, upper_local):
    leaf_size = points.shape[2]
    point_live = jnp.arange(leaf_size, dtype=jnp.int32)[None, :] < counts[:, None]
    masked = jnp.where(point_live[:, None, :], values, jnp.zeros_like(values))
    leaf_coef = jnp.einsum('lcp,lkp->lck', masked.astype(jnp.float32), leaf_basis.astype(jnp.float32)).astype(jnp.bfloat16)
    pairs = leaf_coef.shape[0] // 2
    child_coef = leaf_coef.reshape((pairs, 2) + leaf_coef.shape[1:]).astype(jnp.float32)
    child_transfer = transfer.reshape((pairs, 2) + transfer.shape[1:]).astype(jnp.float32)
    upper_coef = jnp.einsum('pjck,pjkm->pcm', child_coef, child_transfer).astype(jnp.bfloat16)
    upper_ids = (upper_owner * PAR_DEV + upper_local).astype(jnp.int32)
    leaf_ids = (far_owner * LEAF_DEV + far_local).astype(jnp.int32)
    upper_field = far_field(upper_skeleton, upper_coef, upper_ids, PAR_DEV).astype(jnp.bfloat16)
    leaf_far = far_field(leaf_skeleton, leaf_coef, leaf_ids, LEAF_DEV)
    spread = jnp.repeat(upper_field, 2, axis=0)
    leaf_field = (leaf_far + jnp.einsum('lcm,lkm->lck', spread.astype(jnp.float32), transfer.astype(jnp.float32))).astype(jnp.bfloat16)
    far_part = jnp.einsum('lck,lkp->lcp', leaf_field.astype(jnp.float32), leaf_basis.astype(jnp.float32))

    def near_single(target_points, chosen):
        kernel = matern(target_points.astype(jnp.float32)[None], points[chosen].astype(jnp.float32)).astype(jnp.bfloat16)
        return jnp.einsum('jcs,jts->ct', masked[chosen].astype(jnp.float32), kernel.astype(jnp.float32))
    near_part = blocked(near_single, (points, near_list), 4)
    return jnp.where(point_live[:, None, :], far_part + near_part, 0.0)
```

```python
import functools
import math

import jax
import jax.numpy as jnp
from jax import lax
from jax.experimental import pallas as pl
from jax.experimental.pallas import tpu as pltpu
from jax.sharding import PartitionSpec as P

DIM = 8
HALO = 4


SQRT_THREE = 1.7320508075688772
LENGTH_SCALE = 1.5


RATE = SQRT_THREE / LENGTH_SCALE
RATE_TWO = RATE * math.log2(math.e)
BF16 = jnp.bfloat16
F32 = jnp.float32


def matern_of_square(square):
    square = jnp.maximum(square, 1e-30)
    radius = square * lax.rsqrt(square)
    return ((1.0 + RATE * radius) * jnp.exp2(-RATE_TWO * radius)).astype(BF16)


def norm_rows(coords):
    norm = jnp.sum(coords * coords, axis=0, keepdims=True)
    high = norm.astype(BF16).astype(F32)
    middle = (norm - high).astype(BF16).astype(F32)
    low = norm - high - middle
    row = lax.broadcasted_iota(jnp.int32, coords.shape, 0)
    return row, high, middle, low


def source_form(coords):
    row, high, middle, low = norm_rows(coords)
    tail = jnp.where(row == 0, high, jnp.where(row == 1, middle, jnp.where(row == 2, low, 1.0)))
    return jnp.concatenate([coords, jnp.where(row < 6, tail, 0.0)], axis=0)


def target_form(coords):
    row, high, middle, low = norm_rows(coords)
    tail = jnp.where(row == 3, high, jnp.where(row == 4, middle, jnp.where(row == 5, low, 1.0)))
    return jnp.concatenate([-2.0 * coords, jnp.where(row < 6, tail, 0.0)], axis=0)


def near_kernel(near, leaves, ids, pts, cols, out, rows, mine, even, odd):
    half = out.shape[0]
    size = pts.shape[2]
    base = ids[half * near]

    def stage(q, carry):
        rows[q] = source_form(pts[q].astype(F32)).T.astype(BF16)
        return carry

    lax.fori_loop(0, leaves, stage, 0)

    def stage_target(i, carry):
        mine[i] = target_form(pts[base + i].astype(F32)).astype(BF16)
        return carry

    lax.fori_loop(0, half, stage_target, 0)

    def values(i, j, store):
        square = jnp.dot(rows[ids[i * near + j]], mine[i], preferred_element_type=F32)
        store[size * j : size * (j + 1), :] = matern_of_square(square)

    def phase(current, previous, store, ready):
        total = jnp.zeros((cols.shape[1], size), F32)
        for j in range(near):
            values(current, j, store)
            total = total + jnp.dot(
                cols[ids[previous * near + j]],
                ready[size * j : size * (j + 1), :],
                preferred_element_type=F32,
            )
        out[previous] = total

    for j in range(near):
        values(0, j, even)

    def step(k, carry):
        phase(2 * k + 1, 2 * k, odd, even)
        phase(jnp.minimum(2 * k + 2, half - 1), 2 * k + 1, even, odd)
        return carry

    lax.fori_loop(0, half // 2, step, 0)


def near_field(ids, pts, cols, half, near):
    leaves, _, size = pts.shape
    vmem = pl.BlockSpec(memory_space=pltpu.VMEM)
    return pl.pallas_call(
        functools.partial(near_kernel, near, leaves),
        out_shape=jax.ShapeDtypeStruct((half, cols.shape[1], size), F32),
        in_specs=[pl.BlockSpec(memory_space=pltpu.SMEM), vmem, vmem],
        out_specs=vmem,
        scratch_shapes=[
            pltpu.VMEM((leaves, size, 2 * DIM), BF16),
            pltpu.VMEM((half, 2 * DIM, size), BF16),
            pltpu.VMEM((near * size, size), BF16),
            pltpu.VMEM((near * size, size), BF16),
        ],
        compiler_params=pltpu.CompilerParams(vmem_limit_bytes=40 * 2**20),
        cost_estimate=pl.CostEstimate(
            flops=half * near * size * size * 64, bytes_accessed=4 * 2**20, transcendentals=0
        ),
        name="near",
    )(ids, pts, cols)


def with_halo(cells, sides, width):
    for axis, dim in sides:
        count = lax.axis_size(axis)
        ends = count - 1
        head = lax.slice_in_dim(cells, 0, width, axis=dim)
        tail = lax.slice_in_dim(cells, cells.shape[dim] - width, cells.shape[dim], axis=dim)
        cells = jnp.concatenate(
            [
                lax.ppermute(tail, axis, [(i, (i + 1) % count) for i in range(ends)]),
                cells,
                lax.ppermute(head, axis, [((i + 1) % count, i) for i in range(ends)]),
            ],
            axis=dim,
        )
    return cells


def matern(targets, sources):
    square = 0.0
    for coord in range(targets.shape[-2]):
        offset = targets[..., coord, :, None] - sources[..., coord, None, :]
        square = square + offset * offset
    scaled = SQRT_THREE / LENGTH_SCALE * jnp.sqrt(square)
    return (1.0 + scaled) * jnp.exp(-scaled)


def far_sum(target_skel, source_skel, source_coef):
    kernel = matern(
        target_skel.astype(jnp.float32)[:, None], source_skel.astype(jnp.float32)
    ).astype(jnp.bfloat16)
    return jnp.einsum("nfcb,nfab->nca", source_coef, kernel, preferred_element_type=jnp.float32)


def slot_table(owner, local, owners, capacity):
    flat_owner = owner.reshape(-1)
    flat_local = local.reshape(-1)
    owner_hits = (flat_owner[:, None] == jnp.arange(owners, dtype=jnp.int32)[None, :]).astype(
        jnp.int32
    )
    before = jnp.cumsum(owner_hits, axis=0) - owner_hits
    slot_index = jnp.sum(before * owner_hits, axis=1)
    wanted = jnp.zeros((owners, capacity), jnp.int32).at[flat_owner, slot_index].set(flat_local)
    return (wanted, flat_owner, slot_index)


def body(
    points,
    values,
    counts,
    leaf_basis,
    transfer,
    leaf_skeleton,
    upper_skeleton,
    near_list,
    far_owner,
    far_local,
    upper_owner,
    upper_local,
):
    leaf_dev = points.shape[0]
    leaf_size = points.shape[2]
    columns = values.shape[1]
    rank = leaf_basis.shape[1]
    far_count = far_owner.shape[1]
    par_dev = leaf_dev // 2
    owners = lax.axis_size("leaf")
    point_live = lax.broadcasted_iota(jnp.int32, (leaf_dev, leaf_size), 1) < counts[:, None]
    masked = jnp.where(point_live[:, None, :], values, jnp.zeros_like(values))
    leaf_coef = jnp.einsum(
        "lcp,lkp->lck", masked, leaf_basis, preferred_element_type=jnp.float32
    ).astype(jnp.bfloat16)
    child_coef = leaf_coef.reshape(par_dev, 2, columns, rank)
    child_transfer = transfer.reshape(par_dev, 2, rank, rank)
    upper_coef = jnp.einsum(
        "pjck,pjkm->pcm", child_coef, child_transfer, preferred_element_type=jnp.float32
    ).astype(jnp.bfloat16)
    bundle = jnp.concatenate([points, masked], axis=1)
    extended = with_halo(bundle, (("leaf", 0),), HALO)
    first_leaf = lax.axis_index("leaf") * leaf_dev - HALO
    near_count = near_list.shape[1]
    half = leaf_dev // 2
    core = lax.axis_index("rhs")
    swap = [(0, 1), (1, 0)]
    own = extended[:, DIM:]
    cols = jnp.concatenate([own, lax.ppermute(own, "rhs", swap)], axis=1)
    chosen = lax.dynamic_slice_in_dim(near_list - first_leaf, core * half, half, axis=0)
    ids = jnp.concatenate([chosen.reshape(-1), (core * half + HALO)[None]]).astype(jnp.int32)
    near_half = near_field(ids, extended[:, :DIM], cols, half, near_count)
    near_mine = near_half[:, :columns]
    near_theirs = lax.ppermute(near_half[:, columns:], "rhs", swap)
    near_part = jnp.where(
        core == 0,
        jnp.concatenate([near_mine, near_theirs], axis=0),
        jnp.concatenate([near_theirs, near_mine], axis=0),
    )
    leaf_rows = leaf_coef.reshape(leaf_dev, columns * rank)
    leaf_skel_rows = leaf_skeleton.reshape(leaf_dev, DIM * rank)
    capacity = max(2, 2 * leaf_dev * far_count // owners)
    wanted, flat_owner, slot_index = slot_table(far_owner, far_local, owners, capacity)
    asked = lax.all_to_all(wanted, "leaf", split_axis=0, concat_axis=0, tiled=True)
    got_coef = lax.all_to_all(leaf_rows[asked], "leaf", split_axis=0, concat_axis=0, tiled=True)
    got_skel = lax.all_to_all(
        leaf_skel_rows[asked], "leaf", split_axis=0, concat_axis=0, tiled=True
    )
    picked_coef = got_coef[flat_owner, slot_index]
    picked_skel = got_skel[flat_owner, slot_index]
    leaf_far = far_sum(
        leaf_skeleton,
        picked_skel.reshape(leaf_dev, far_count, DIM, rank),
        picked_coef.reshape(leaf_dev, far_count, columns, rank),
    )
    upper_rows = upper_coef.reshape(par_dev, columns * rank)
    upper_skel_rows = upper_skeleton.reshape(par_dev, DIM * rank)
    upper_capacity = max(2, 2 * par_dev * far_count // owners)
    upper_wanted, upper_flat, upper_slot = slot_table(
        upper_owner, upper_local, owners, upper_capacity
    )
    asked = lax.all_to_all(upper_wanted, "leaf", split_axis=0, concat_axis=0, tiled=True)
    got_upper = lax.all_to_all(upper_rows[asked], "leaf", split_axis=0, concat_axis=0, tiled=True)
    got_upper_skel = lax.all_to_all(
        upper_skel_rows[asked], "leaf", split_axis=0, concat_axis=0, tiled=True
    )
    chosen_coef = got_upper[upper_flat, upper_slot]
    chosen_skel = got_upper_skel[upper_flat, upper_slot]
    upper_field = far_sum(
        upper_skeleton,
        chosen_skel.reshape(par_dev, far_count, DIM, rank),
        chosen_coef.reshape(par_dev, far_count, columns, rank),
    ).astype(jnp.bfloat16)
    spread = jnp.repeat(upper_field, 2, axis=0)
    leaf_field = (
        leaf_far + jnp.einsum("lcm,lkm->lck", spread, transfer, preferred_element_type=jnp.float32)
    ).astype(jnp.bfloat16)
    far_part = jnp.einsum(
        "lck,lkp->lcp", leaf_field, leaf_basis, preferred_element_type=jnp.float32
    )
    return jnp.where(point_live[:, None, :], far_part + near_part, 0.0)


def solution(mesh):
    return jax.shard_map(
        body,
        mesh=mesh,
        in_specs=(
            P("leaf", None, None),
            P("leaf", "rhs", None),
            P("leaf"),
            P("leaf", None, None),
            P("leaf", None, None),
            P("leaf", None, None),
            P("leaf", None, None),
            P("leaf", None),
            P("leaf", None),
            P("leaf", None),
            P("leaf", None),
            P("leaf", None),
        ),
        out_specs=P("leaf", "rhs", None),
        check_vma=False,
    )
```

```python
import functools
import math

import jax
import jax.numpy as jnp
from jax import lax
from jax.experimental import pallas as pl
from jax.experimental.pallas import tpu as pltpu
from jax.sharding import PartitionSpec as P

DIM = 8
HALO = 4


SQRT_THREE = 1.7320508075688772
LENGTH_SCALE = 1.5


RATE = SQRT_THREE / LENGTH_SCALE
RATE_TWO = RATE * math.log2(math.e)
BF16 = jnp.bfloat16
F32 = jnp.float32


def matern_of_square(square):
    square = jnp.maximum(square, 1e-30)
    radius = square * lax.rsqrt(square)
    return ((1.0 + RATE * radius) * jnp.exp2(-RATE_TWO * radius)).astype(BF16)


def norm_rows(coords):
    norm = jnp.sum(coords * coords, axis=0, keepdims=True)
    high = norm.astype(BF16).astype(F32)
    middle = (norm - high).astype(BF16).astype(F32)
    low = norm - high - middle
    row = lax.broadcasted_iota(jnp.int32, coords.shape, 0)
    return row, high, middle, low


def source_form(coords):
    row, high, middle, low = norm_rows(coords)
    tail = jnp.where(row == 0, high, jnp.where(row == 1, middle, jnp.where(row == 2, low, 1.0)))
    return jnp.concatenate([coords, jnp.where(row < 6, tail, 0.0)], axis=0)


def target_form(coords):
    row, high, middle, low = norm_rows(coords)
    tail = jnp.where(row == 3, high, jnp.where(row == 4, middle, jnp.where(row == 5, low, 1.0)))
    return jnp.concatenate([-2.0 * coords, jnp.where(row < 6, tail, 0.0)], axis=0)


def near_kernel(near, leaves, ids, pts, cols, out, rows, mine, even, odd):
    half = out.shape[0]
    size = pts.shape[2]
    base = ids[half * near]

    def stage(q, carry):
        rows[q] = source_form(pts[q].astype(F32)).T.astype(BF16)
        return carry

    lax.fori_loop(0, leaves, stage, 0)

    def stage_target(i, carry):
        mine[i] = target_form(pts[base + i].astype(F32)).astype(BF16)
        return carry

    lax.fori_loop(0, half, stage_target, 0)

    def values(i, j, store):
        square = jnp.dot(rows[ids[i * near + j]], mine[i], preferred_element_type=F32)
        store[size * j : size * (j + 1), :] = matern_of_square(square)

    def phase(current, previous, store, ready):
        total = jnp.zeros((cols.shape[1], size), F32)
        for j in range(near):
            values(current, j, store)
            total = total + jnp.dot(
                cols[ids[previous * near + j]],
                ready[size * j : size * (j + 1), :],
                preferred_element_type=F32,
            )
        out[previous] = total

    for j in range(near):
        values(0, j, even)

    def step(k, carry):
        phase(2 * k + 1, 2 * k, odd, even)
        phase(jnp.minimum(2 * k + 2, half - 1), 2 * k + 1, even, odd)
        return carry

    lax.fori_loop(0, half // 2, step, 0)


def near_field(ids, pts, cols, half, near):
    leaves, _, size = pts.shape
    vmem = pl.BlockSpec(memory_space=pltpu.VMEM)
    return pl.pallas_call(
        functools.partial(near_kernel, near, leaves),
        out_shape=jax.ShapeDtypeStruct((half, cols.shape[1], size), F32),
        in_specs=[pl.BlockSpec(memory_space=pltpu.SMEM), vmem, vmem],
        out_specs=vmem,
        scratch_shapes=[
            pltpu.VMEM((leaves, size, 2 * DIM), BF16),
            pltpu.VMEM((half, 2 * DIM, size), BF16),
            pltpu.VMEM((near * size, size), BF16),
            pltpu.VMEM((near * size, size), BF16),
        ],
        compiler_params=pltpu.CompilerParams(vmem_limit_bytes=40 * 2**20),
        cost_estimate=pl.CostEstimate(
            flops=half * near * size * size * 64, bytes_accessed=4 * 2**20, transcendentals=0
        ),
        name="near",
    )(ids, pts, cols)


def with_halo(cells, sides, width):
    for axis, dim in sides:
        count = lax.axis_size(axis)
        ends = count - 1
        head = lax.slice_in_dim(cells, 0, width, axis=dim)
        tail = lax.slice_in_dim(cells, cells.shape[dim] - width, cells.shape[dim], axis=dim)
        cells = jnp.concatenate(
            [
                lax.ppermute(tail, axis, [(i, (i + 1) % count) for i in range(ends)]),
                cells,
                lax.ppermute(head, axis, [((i + 1) % count, i) for i in range(ends)]),
            ],
            axis=dim,
        )
    return cells


SIDE = 4


def coef_kernel(values, basis, transfer, leaf_skel, upper_skel, table):
    pairs = leaf_skel.shape[0] // 2
    step_pairs = 4

    def step(i, carry):
        upper = []
        for n in range(step_pairs):
            p = i * step_pairs + n
            halves = [
                lax.dot_general(
                    values[2 * p + k],
                    basis[2 * p + k],
                    (((1,), (1,)), ((), ())),
                    preferred_element_type=F32,
                )
                for k in range(2)
            ]
            coef = jnp.concatenate(halves, axis=1)
            skel = [leaf_skel[2 * p + k].astype(F32) for k in range(2)]
            table[p] = jnp.concatenate([jnp.concatenate(skel, axis=1), coef], axis=0).astype(BF16)
            stacked = jnp.concatenate([transfer[2 * p], transfer[2 * p + 1]], axis=0)
            upper.append(jnp.dot(coef.astype(BF16), stacked, preferred_element_type=F32))
        for n in range(step_pairs // 2):
            p = i * (step_pairs // 2) + n
            skel = [upper_skel[2 * p + k].astype(F32) for k in range(2)]
            coef = jnp.concatenate(upper[2 * n : 2 * n + 2], axis=1)
            table[pairs + p] = jnp.concatenate(
                [jnp.concatenate(skel, axis=1), coef], axis=0
            ).astype(BF16)
        return carry

    lax.fori_loop(0, pairs // step_pairs, step, 0)


def far_kernel(units, rows_each, *refs):
    pieces, refs = refs[:10], refs[10:]
    skels, lists, outs = refs[:4], refs[4:8], refs[8:12]
    table, sums, sems = refs[12:]
    block = SIDE * rows_each
    copies = []
    for n, piece in enumerate(pieces):
        order, part = divmod(n, 5)
        start = order * SIDE * block + min(part, 3) * block
        if part == 3:
            where, size = table.at[pl.ds(start, block // 2)], block // 2
        elif part == 4:
            where, size = table.at[pl.ds(start + block // 2, block // 2)], block // 2
        else:
            where, size = table.at[pl.ds(start, block)], block
        copy = pltpu.make_async_copy(piece, where, sems.at[n])
        copy.start()
        copies.append(copy)
    targets = 2 * skels[0].shape[0]
    rank = skels[0].shape[2] // 2
    lane = lax.broadcasted_iota(jnp.int32, (DIM, 2 * rank), 1)
    low = lane < rank

    def clear(i, carry):
        sums[i] = jnp.zeros(sums.shape[1:], F32)
        return carry

    lax.fori_loop(0, sums.shape[0], clear, 0)
    for copy in copies:
        copy.wait()

    def turned(array):
        return jnp.concatenate([array[:, rank:], array[:, :rank]], axis=1)

    for r in range(4):
        skel, listed, first = skels[r], lists[r], r * (targets + 1)

        def step(i, carry):
            for quad in range(units // 4):
                where, left, right, coefs = [], [], [], []
                for n in range(4):
                    entry = listed[i * units + quad * 4 + n]
                    target = entry >> 12
                    row = (entry >> 1) & 2047
                    source = table[row].astype(F32)
                    swap = (entry & 1) != (n % 2)
                    source = jnp.where(swap, turned(source), source)
                    keep = low if n % 2 == 0 else jnp.logical_not(low)
                    form = jnp.where(
                        jnp.concatenate([keep, keep], axis=0), source_form(source[:DIM]), 0.0
                    )
                    coef = jnp.where(keep, source[DIM:], 0.0)
                    blank = jnp.zeros_like(form)
                    empty = jnp.zeros_like(coef)
                    wide = [form, blank] if n < 2 else [blank, form]
                    right.append(jnp.concatenate(wide, axis=1))
                    wide = [coef, empty] if n < 2 else [empty, coef]
                    coefs.append(jnp.concatenate(wide, axis=1))
                    pair = skel[jnp.minimum(target, targets - 1) >> 1].astype(F32)
                    pair = jnp.where((target & 1) == 1, turned(pair), pair)
                    left.append(target_form(pair))
                    where.append(first + target)
                left = jnp.concatenate(left, axis=0)[:, :rank].astype(BF16)
                right = jnp.concatenate(right, axis=0).astype(BF16)
                square = lax.dot_general(
                    left, right, (((0,), (0,)), ((), ())), preferred_element_type=F32
                )
                fields = lax.dot_general(
                    jnp.concatenate(coefs, axis=0).astype(BF16),
                    matern_of_square(square),
                    (((1,), (1,)), ((), ())),
                    preferred_element_type=F32,
                )
                for n in range(4):
                    sums[where[n]] += fields[DIM * n : DIM * (n + 1)]
            return carry

        count = listed[listed.shape[0] - 128]
        lax.fori_loop(0, (count + units - 1) // units, step, 0)

        def pack(p, carry):
            outs[r][p] = jnp.concatenate([sums[first + 2 * p], sums[first + 2 * p + 1]], axis=1)
            return carry

        lax.fori_loop(0, targets // 2, pack, 0)


def final_kernel(counts, transfer, basis, near_mine, near_theirs, *refs):
    parts, out = refs[:4], refs[4]
    leaves = out.shape[0]
    half = leaves // 2
    rank = transfer.shape[1]
    core = counts[leaves]
    lane = lax.broadcasted_iota(jnp.int32, out.shape[1:], 1)

    def total(p):
        return (parts[0][p] + parts[1][p]) + (parts[2][p] + parts[3][p])

    def step(i, carry):
        for n in range(2):
            upper = total(half + 2 * i + n).astype(BF16)
            for m in range(2):
                pair = 4 * i + 2 * n + m
                field = total(pair)
                for k in range(2):
                    leaf = 2 * pair + k
                    down = lax.dot_general(
                        upper[:, m * rank : (m + 1) * rank],
                        transfer[leaf],
                        (((1,), (1,)), ((), ())),
                        preferred_element_type=F32,
                    )
                    here = (field[:, k * rank : (k + 1) * rank] + down).astype(BF16)
                    result = jnp.dot(here, basis[leaf], preferred_element_type=F32)
                    owner = leaf // half
                    inner = leaf - owner * half
                    near = jnp.where(
                        owner == core, near_mine[inner][: out.shape[1]], near_theirs[inner]
                    )
                    out[leaf] = jnp.where(lane < counts[leaf], result + near, 0.0)
        return carry

    lax.fori_loop(0, leaves // 8, step, 0)


def z_shift(r):
    return [
        (SIDE * k + z, SIDE * k + (z - r) % SIDE) for k in range(SIDE * SIDE) for z in range(SIDE)
    ]


def line_gather(block, axis):
    stride = SIDE * SIDE if axis == 0 else SIDE

    def moved(array, by):
        pairs = []
        for i in range(SIDE**3):
            at = i // stride % SIDE
            pairs.append((i, i + ((at + by) % SIDE - at) * stride))
        return lax.ppermute(array, "leaf", pairs)

    cut = block.shape[0] // 2
    ahead, behind = moved(block, -1), moved(block, 1)
    return [block, ahead, behind, moved(behind[:cut], 1), moved(ahead[cut:], -1)]


def plane_gather(block, axes):
    first = line_gather(block, axes[0])
    return line_gather(jnp.concatenate(first, axis=0), axes[1])


def unit_lists(leaf_owner, leaf_local, upper_owner, upper_local, rows_each, capacity):
    me = lax.axis_index("leaf")
    leaves, far = leaf_owner.shape
    parents = upper_owner.shape[0]
    owner = jnp.concatenate([leaf_owner.reshape(-1), upper_owner.reshape(-1)])
    local = jnp.concatenate([leaf_local.reshape(-1), leaves + upper_local.reshape(-1)])
    target = jnp.arange((leaves + parents) * far, dtype=jnp.int32) // far

    def slot(offset):
        return jnp.where(offset == 2, 3, jnp.where(offset == 3, 2, offset))

    x = slot((owner // (SIDE * SIDE) - me // (SIDE * SIDE)) % SIDE)
    y = slot((owner // SIDE - me // SIDE) % SIDE)
    pair = local // 2
    in_first = pair < rows_each
    row = jnp.where(
        in_first,
        (x * SIDE + y) * rows_each + pair,
        SIDE * SIDE * rows_each + (y * SIDE + x) * rows_each + pair - rows_each,
    )
    code = (target << 12) | (row << 1) | (local & 1)
    hits = (owner[:, None] % SIDE == jnp.arange(SIDE, dtype=jnp.int32)[None, :]).astype(BF16)
    number = owner.shape[0]
    order = jnp.arange(number, dtype=jnp.int32)
    before = (order[None, :] < order[:, None]).astype(BF16)
    rank = jnp.sum(jnp.dot(before, hits, preferred_element_type=F32) * hits.astype(F32), axis=1)
    spot = (rank.astype(jnp.int32)[:, None] == jnp.arange(capacity, dtype=jnp.int32)[None, :]).astype(
        BF16
    )
    digits = jnp.stack(
        [(code & 127), ((code >> 7) & 127), (code >> 14), jnp.ones_like(code)], axis=0
    ).astype(BF16)
    weights = (hits.T[:, None, :] * digits[None]).reshape(SIDE * 4, number)
    found = jnp.dot(weights, spot, preferred_element_type=F32).astype(jnp.int32)
    found = found.reshape(SIDE, 4, capacity)
    codes = found[:, 0] + (found[:, 1] << 7) + (found[:, 2] << 14)
    codes = codes + jnp.where(found[:, 3] == 0, (leaves + parents) << 12, 0)
    counts = jnp.sum(found[:, 3], axis=1)
    return jnp.concatenate([codes, jnp.broadcast_to(counts[:, None], (SIDE, 128))], axis=1)


def body(
    points,
    values,
    counts,
    leaf_basis,
    transfer,
    leaf_skeleton,
    upper_skeleton,
    near_list,
    far_owner,
    far_local,
    upper_owner,
    upper_local,
):
    leaf_dev = points.shape[0]
    leaf_size = points.shape[2]
    columns = values.shape[1]
    rank = leaf_basis.shape[1]
    near_count = near_list.shape[1]
    half = leaf_dev // 2
    pairs = leaf_dev // 2 + leaf_dev // 4
    rows_each = pairs // 2
    capacity = leaf_dev * far_owner.shape[1] * 3 // 4
    me = lax.axis_index("leaf")
    core = lax.axis_index("rhs")
    swap = [(0, 1), (1, 0)]
    vmem = pl.BlockSpec(memory_space=pltpu.VMEM)
    smem = pl.BlockSpec(memory_space=pltpu.SMEM)
    anywhere = pl.BlockSpec(memory_space=pl.ANY)
    params = pltpu.CompilerParams(vmem_limit_bytes=40 * 2**20)

    point_live = lax.broadcasted_iota(jnp.int32, (leaf_dev, leaf_size), 1) < counts[:, None]
    masked = jnp.where(point_live[:, None, :], values, jnp.zeros_like(values))
    table = pl.pallas_call(
        coef_kernel,
        out_shape=jax.ShapeDtypeStruct((pairs, 2 * DIM, 2 * rank), BF16),
        in_specs=[vmem] * 5,
        out_specs=vmem,
        compiler_params=params,
        cost_estimate=pl.CostEstimate(flops=10**8, bytes_accessed=6 * 2**20, transcendentals=0),
        name="coef",
    )(masked, leaf_basis, transfer, leaf_skeleton, upper_skeleton)
    pieces = plane_gather(table[:rows_each], (1, 0)) + plane_gather(table[rows_each:], (0, 1))

    lists = unit_lists(far_owner, far_local, upper_owner, upper_local, rows_each, capacity)
    skel = table[:, :DIM]
    all_lists, all_skels = [lists[me % SIDE]], [skel]
    for r in range(1, SIDE):
        all_lists.append(lax.ppermute(lists[(me - r) % SIDE], "leaf", z_shift(r)))
        all_skels.append(lax.ppermute(skel, "leaf", z_shift(r)))

    bundle = jnp.concatenate([points, masked], axis=1)
    extended = with_halo(bundle, (("leaf", 0),), HALO)
    own = extended[:, DIM:]
    cols = jnp.concatenate([own, lax.ppermute(own, "rhs", swap)], axis=1)
    first_leaf = me * leaf_dev - HALO
    chosen = lax.dynamic_slice_in_dim(near_list - first_leaf, core * half, half, axis=0)
    ids = jnp.concatenate([chosen.reshape(-1), (core * half + HALO)[None]]).astype(jnp.int32)
    near_half = near_field(ids, extended[:, :DIM], cols, half, near_count)
    near_theirs = lax.ppermute(near_half[:, columns:], "rhs", swap)

    part = jax.ShapeDtypeStruct((pairs, columns, 2 * rank), F32)
    parts = pl.pallas_call(
        functools.partial(far_kernel, 16, rows_each),
        out_shape=[part] * 4,
        in_specs=[anywhere] * 10 + [vmem] * 4 + [smem] * 4,
        out_specs=[vmem] * 4,
        scratch_shapes=[
            pltpu.VMEM((2 * SIDE * SIDE * rows_each, 2 * DIM, 2 * rank), BF16),
            pltpu.VMEM((4 * (2 * pairs + 1), columns, rank), F32),
            pltpu.SemaphoreType.DMA((10,)),
        ],
        compiler_params=params,
        cost_estimate=pl.CostEstimate(
            flops=3 * 10**10, bytes_accessed=10 * 2**20, transcendentals=0
        ),
        name="far",
    )(*pieces, *all_skels, *all_lists)
    mine = [parts[0]]
    for r in range(1, SIDE):
        mine.append(lax.ppermute(parts[r], "leaf", z_shift(-r)))

    limits = jnp.concatenate([counts, core[None]]).astype(jnp.int32)
    return pl.pallas_call(
        final_kernel,
        out_shape=jax.ShapeDtypeStruct((leaf_dev, columns, leaf_size), F32),
        in_specs=[smem] + [vmem] * 8,
        out_specs=vmem,
        compiler_params=params,
        name="final",
    )(limits, transfer, leaf_basis, near_half, near_theirs, *mine)


def solution(mesh):
    return jax.shard_map(
        body,
        mesh=mesh,
        in_specs=(
            P("leaf", None, None),
            P("leaf", "rhs", None),
            P("leaf"),
            P("leaf", None, None),
            P("leaf", None, None),
            P("leaf", None, None),
            P("leaf", None, None),
            P("leaf", None),
            P("leaf", None),
            P("leaf", None),
            P("leaf", None),
            P("leaf", None),
        ),
        out_specs=P("leaf", "rhs", None),
        check_vma=False,
    )
```

```python
import functools
import math

import jax
import jax.numpy as jnp
from jax import lax
from jax.experimental import pallas as pl
from jax.experimental.pallas import tpu as pltpu
from jax.sharding import PartitionSpec as P

DIM = 8
HALO = 4


SQRT_THREE = 1.7320508075688772
LENGTH_SCALE = 1.5


RATE = SQRT_THREE / LENGTH_SCALE
RATE_TWO = RATE * math.log2(math.e)
BF16 = jnp.bfloat16
F32 = jnp.float32


def matern_of_square(square):
    square = jnp.maximum(square, 1e-30)
    radius = square * lax.rsqrt(square)
    return ((1.0 + RATE * radius) * jnp.exp2(-RATE_TWO * radius)).astype(BF16)


def norm_rows(coords):
    norm = jnp.sum(coords * coords, axis=0, keepdims=True)
    high = norm.astype(BF16).astype(F32)
    middle = (norm - high).astype(BF16).astype(F32)
    low = norm - high - middle
    row = lax.broadcasted_iota(jnp.int32, coords.shape, 0)
    return row, high, middle, low


def source_form(coords):
    row, high, middle, low = norm_rows(coords)
    tail = jnp.where(row == 0, high, jnp.where(row == 1, middle, jnp.where(row == 2, low, 1.0)))
    return jnp.concatenate([coords, jnp.where(row < 6, tail, 0.0)], axis=0)


def target_form(coords):
    row, high, middle, low = norm_rows(coords)
    tail = jnp.where(row == 3, high, jnp.where(row == 4, middle, jnp.where(row == 5, low, 1.0)))
    return jnp.concatenate([-2.0 * coords, jnp.where(row < 6, tail, 0.0)], axis=0)


def near_kernel(near, leaves, ids, pts, cols, out, rows, mine, even, odd):
    half = out.shape[0]
    size = pts.shape[2]
    base = ids[half * near]

    def stage(q, carry):
        rows[q] = source_form(pts[q].astype(F32)).T.astype(BF16)
        return carry

    lax.fori_loop(0, leaves, stage, 0)

    def stage_target(i, carry):
        mine[i] = target_form(pts[base + i].astype(F32)).astype(BF16)
        return carry

    lax.fori_loop(0, half, stage_target, 0)

    def values(i, j, store):
        square = jnp.dot(rows[ids[i * near + j]], mine[i], preferred_element_type=F32)
        store[size * j : size * (j + 1), :] = matern_of_square(square)

    def phase(current, previous, store, ready):
        total = jnp.zeros((cols.shape[1], size), F32)
        for j in range(near):
            values(current, j, store)
            total = total + jnp.dot(
                cols[ids[previous * near + j]],
                ready[size * j : size * (j + 1), :],
                preferred_element_type=F32,
            )
        out[previous] = total

    for j in range(near):
        values(0, j, even)

    def step(k, carry):
        phase(2 * k + 1, 2 * k, odd, even)
        phase(jnp.minimum(2 * k + 2, half - 1), 2 * k + 1, even, odd)
        return carry

    lax.fori_loop(0, half // 2, step, 0)


def near_field(ids, pts, cols, half, near):
    leaves, _, size = pts.shape
    vmem = pl.BlockSpec(memory_space=pltpu.VMEM)
    return pl.pallas_call(
        functools.partial(near_kernel, near, leaves),
        out_shape=jax.ShapeDtypeStruct((half, cols.shape[1], size), F32),
        in_specs=[pl.BlockSpec(memory_space=pltpu.SMEM), vmem, vmem],
        out_specs=vmem,
        scratch_shapes=[
            pltpu.VMEM((leaves, size, 2 * DIM), BF16),
            pltpu.VMEM((half, 2 * DIM, size), BF16),
            pltpu.VMEM((near * size, size), BF16),
            pltpu.VMEM((near * size, size), BF16),
        ],
        compiler_params=pltpu.CompilerParams(vmem_limit_bytes=40 * 2**20),
        cost_estimate=pl.CostEstimate(
            flops=half * near * size * size * 64, bytes_accessed=4 * 2**20, transcendentals=0
        ),
        name="near",
    )(ids, pts, cols)


def with_halo(cells, sides, width):
    for axis, dim in sides:
        count = lax.axis_size(axis)
        ends = count - 1
        head = lax.slice_in_dim(cells, 0, width, axis=dim)
        tail = lax.slice_in_dim(cells, cells.shape[dim] - width, cells.shape[dim], axis=dim)
        cells = jnp.concatenate(
            [
                lax.ppermute(tail, axis, [(i, (i + 1) % count) for i in range(ends)]),
                cells,
                lax.ppermute(head, axis, [((i + 1) % count, i) for i in range(ends)]),
            ],
            axis=dim,
        )
    return cells


SIDE = 4


def coef_kernel(values, basis, transfer, leaf_skel, upper_skel, table):
    pairs = leaf_skel.shape[0] // 2
    step_pairs = 8

    def step(i, carry):
        first = i * step_pairs
        coefs = [
            lax.dot_general(
                values[2 * first + n],
                basis[2 * first + n],
                (((1,), (1,)), ((), ())),
                preferred_element_type=F32,
            )
            for n in range(2 * step_pairs)
        ]
        coefs = [jnp.concatenate(coefs[2 * n : 2 * n + 2], axis=1) for n in range(step_pairs)]
        upper = []
        for n in range(step_pairs):
            p = first + n
            stacked = jnp.concatenate([transfer[2 * p], transfer[2 * p + 1]], axis=0)
            upper.append(jnp.dot(coefs[n].astype(BF16), stacked, preferred_element_type=F32))
        for n in range(step_pairs):
            p = first + n
            skel = [leaf_skel[2 * p + k].astype(F32) for k in range(2)]
            table[p] = jnp.concatenate(
                [jnp.concatenate(skel, axis=1), coefs[n]], axis=0
            ).astype(BF16)
        for n in range(step_pairs // 2):
            p = i * (step_pairs // 2) + n
            skel = [upper_skel[2 * p + k].astype(F32) for k in range(2)]
            coef = jnp.concatenate(upper[2 * n : 2 * n + 2], axis=1)
            table[pairs + p] = jnp.concatenate(
                [jnp.concatenate(skel, axis=1), coef], axis=0
            ).astype(BF16)
        return carry

    lax.fori_loop(0, pairs // step_pairs, step, 0)


def far_kernel(units, listed, first_half, second_half, skels, outs, table, sums, sems):
    block = first_half.shape[0]
    copies = [
        pltpu.make_async_copy(first_half, table.at[pl.ds(0, block)], sems.at[0]),
        pltpu.make_async_copy(second_half, table.at[pl.ds(block, block)], sems.at[1]),
    ]
    for copy in copies:
        copy.start()
    targets = 2 * skels.shape[1]
    rank = skels.shape[3] // 2
    lane = lax.broadcasted_iota(jnp.int32, (DIM, 2 * rank), 1)
    low = lane < rank

    def clear(i, carry):
        sums[i] = jnp.zeros(sums.shape[1:], F32)
        return carry

    lax.fori_loop(0, sums.shape[0], clear, 0)
    for copy in copies:
        copy.wait()

    def turned(array):
        return jnp.concatenate([array[:, rank:], array[:, :rank]], axis=1)

    for r in range(SIDE):
        first = r * (targets + 1)

        def step(i, carry):
            where, squares, weights = [], [], []
            for quad in range(units // 4):
                left, right, coefs = [], [], []
                for n in range(4):
                    entry = listed[r, i * units + quad * 4 + n]
                    target = entry >> 12
                    row = (entry >> 1) & 2047
                    source = table[row].astype(F32)
                    swap = (entry & 1) != (n % 2)
                    source = jnp.where(swap, turned(source), source)
                    keep = low if n % 2 == 0 else jnp.logical_not(low)
                    form = jnp.where(
                        jnp.concatenate([keep, keep], axis=0), source_form(source[:DIM]), 0.0
                    )
                    coef = jnp.where(keep, source[DIM:], 0.0)
                    blank = jnp.zeros_like(form)
                    empty = jnp.zeros_like(coef)
                    wide = [form, blank] if n < 2 else [blank, form]
                    right.append(jnp.concatenate(wide, axis=1))
                    wide = [coef, empty] if n < 2 else [empty, coef]
                    coefs.append(jnp.concatenate(wide, axis=1))
                    pair = skels[r, jnp.minimum(target, targets - 1) >> 1].astype(F32)
                    pair = jnp.where((target & 1) == 1, turned(pair), pair)
                    left.append(target_form(pair))
                    where.append(first + target)
                left = jnp.concatenate(left, axis=0)[:, :rank].astype(BF16)
                right = jnp.concatenate(right, axis=0).astype(BF16)
                weights.append(jnp.concatenate(coefs, axis=0).astype(BF16))
                squares.append(
                    lax.dot_general(
                        left, right, (((0,), (0,)), ((), ())), preferred_element_type=F32
                    )
                )
            kernels = [matern_of_square(square) for square in squares]
            fields = [
                lax.dot_general(
                    weight, kernel, (((1,), (1,)), ((), ())), preferred_element_type=F32
                )
                for weight, kernel in zip(weights, kernels)
            ]
            for n in range(units):
                at = DIM * (n % 4)
                sums[where[n]] += fields[n // 4][at : at + DIM]
            return carry

        count = listed[r, listed.shape[1] - 128]
        lax.fori_loop(0, (count + units - 1) // units, step, 0)

        def pack(p, carry):
            outs[r, p] = jnp.concatenate([sums[first + 2 * p], sums[first + 2 * p + 1]], axis=1)
            return carry

        lax.fori_loop(0, targets // 2, pack, 0)


def final_kernel(counts, transfer, basis, near_mine, near_theirs, total, out):
    leaves = out.shape[0]
    half = leaves // 2
    rank = transfer.shape[1]
    core = counts[leaves]
    lane = lax.broadcasted_iota(jnp.int32, out.shape[1:], 1)
    group = 16

    def step(i, carry):
        first = i * group
        upper = [total[half + first // 4 + n].astype(BF16) for n in range(group // 4)]
        down = [
            lax.dot_general(
                upper[n // 4][:, (n // 2 % 2) * rank : (n // 2 % 2 + 1) * rank],
                transfer[first + n],
                (((1,), (1,)), ((), ())),
                preferred_element_type=F32,
            )
            for n in range(group)
        ]
        pairs = [total[first // 2 + n] for n in range(group // 2)]
        field = [
            (pairs[n // 2][:, (n % 2) * rank : (n % 2 + 1) * rank] + down[n]).astype(BF16)
            for n in range(group)
        ]
        result = [
            jnp.dot(field[n], basis[first + n], preferred_element_type=F32) for n in range(group)
        ]
        owner = first // half
        inner = first - owner * half
        for n in range(group):
            near = jnp.where(
                owner == core, near_mine[inner + n][: out.shape[1]], near_theirs[inner + n]
            )
            out[first + n] = jnp.where(lane < counts[first + n], result[n] + near, 0.0)
        return carry

    lax.fori_loop(0, leaves // group, step, 0)


def lines(axis):
    stride = (SIDE * SIDE, SIDE, 1)[axis]
    starts = [i for i in range(SIDE**3) if i // stride % SIDE == 0]
    return [[start + stride * k for k in range(SIDE)] for start in starts]


def line_gather(block, axis):
    return lax.all_gather(block, "leaf", axis_index_groups=lines(axis), tiled=True)


def unit_lists(leaf_owner, leaf_local, upper_owner, upper_local, rows_each, capacity):
    leaves, far = leaf_owner.shape
    parents = upper_owner.shape[0]
    owner = jnp.concatenate([leaf_owner.reshape(-1), upper_owner.reshape(-1)])
    local = jnp.concatenate([leaf_local.reshape(-1), leaves + upper_local.reshape(-1)])
    target = jnp.arange((leaves + parents) * far, dtype=jnp.int32) // far

    x = owner // (SIDE * SIDE)
    y = owner // SIDE % SIDE
    pair = local // 2
    in_first = pair < rows_each
    row = jnp.where(
        in_first,
        (x * SIDE + y) * rows_each + pair,
        SIDE * SIDE * rows_each + (y * SIDE + x) * rows_each + pair - rows_each,
    )
    code = (target << 12) | (row << 1) | (local & 1)
    hits = (owner[:, None] % SIDE == jnp.arange(SIDE, dtype=jnp.int32)[None, :]).astype(BF16)
    number = owner.shape[0]
    order = jnp.arange(number, dtype=jnp.int32)
    before = (order[None, :] < order[:, None]).astype(BF16)
    rank = jnp.sum(jnp.dot(before, hits, preferred_element_type=F32) * hits.astype(F32), axis=1)
    spot = (rank.astype(jnp.int32)[:, None] == jnp.arange(capacity, dtype=jnp.int32)[None, :]).astype(
        BF16
    )
    digits = jnp.stack(
        [(code & 127), ((code >> 7) & 127), (code >> 14), jnp.ones_like(code)], axis=0
    ).astype(BF16)
    weights = (hits.T[:, None, :] * digits[None]).reshape(SIDE * 4, number)
    found = jnp.dot(weights, spot, preferred_element_type=F32).astype(jnp.int32)
    found = found.reshape(SIDE, 4, capacity)
    codes = found[:, 0] + (found[:, 1] << 7) + (found[:, 2] << 14)
    codes = codes + jnp.where(found[:, 3] == 0, (leaves + parents) << 12, 0)
    counts = jnp.sum(found[:, 3], axis=1)
    return jnp.concatenate([codes, jnp.broadcast_to(counts[:, None], (SIDE, 128))], axis=1)


def body(
    points,
    values,
    counts,
    leaf_basis,
    transfer,
    leaf_skeleton,
    upper_skeleton,
    near_list,
    far_owner,
    far_local,
    upper_owner,
    upper_local,
):
    leaf_dev = points.shape[0]
    leaf_size = points.shape[2]
    columns = values.shape[1]
    rank = leaf_basis.shape[1]
    near_count = near_list.shape[1]
    half = leaf_dev // 2
    pairs = leaf_dev // 2 + leaf_dev // 4
    rows_each = pairs // 2
    capacity = leaf_dev * far_owner.shape[1] * 3 // 4
    me = lax.axis_index("leaf")
    core = lax.axis_index("rhs")
    swap = [(0, 1), (1, 0)]
    vmem = pl.BlockSpec(memory_space=pltpu.VMEM)
    smem = pl.BlockSpec(memory_space=pltpu.SMEM)
    anywhere = pl.BlockSpec(memory_space=pl.ANY)
    params = pltpu.CompilerParams(vmem_limit_bytes=40 * 2**20)

    point_live = lax.broadcasted_iota(jnp.int32, (leaf_dev, leaf_size), 1) < counts[:, None]
    masked = jnp.where(point_live[:, None, :], values, jnp.zeros_like(values))
    table = pl.pallas_call(
        coef_kernel,
        out_shape=jax.ShapeDtypeStruct((pairs, 2 * DIM, 2 * rank), BF16),
        in_specs=[vmem] * 5,
        out_specs=vmem,
        compiler_params=params,
        cost_estimate=pl.CostEstimate(flops=10**8, bytes_accessed=6 * 2**20, transcendentals=0),
        name="coef",
    )(masked, leaf_basis, transfer, leaf_skeleton, upper_skeleton)
    first_half = line_gather(line_gather(table[:rows_each], 1), 0)
    second_half = line_gather(line_gather(table[rows_each:], 0), 1)
    lists = unit_lists(far_owner, far_local, upper_owner, upper_local, rows_each, capacity)
    lists = line_gather(lists, 2).reshape(SIDE, SIDE, -1)
    lists = lax.dynamic_index_in_dim(lists, me % SIDE, axis=1, keepdims=False)
    skels = line_gather(table[:, :DIM], 2).reshape(SIDE, pairs, DIM, 2 * rank)

    bundle = jnp.concatenate([points, masked], axis=1)
    extended = with_halo(bundle, (("leaf", 0),), HALO)
    own = extended[:, DIM:]
    cols = jnp.concatenate([own, lax.ppermute(own, "rhs", swap)], axis=1)
    first_leaf = me * leaf_dev - HALO
    chosen = lax.dynamic_slice_in_dim(near_list - first_leaf, core * half, half, axis=0)
    start = core * half + HALO
    early = half * 3 // 4

    def near_ids(rows, offset):
        return jnp.concatenate([rows.reshape(-1), (start + offset)[None]]).astype(jnp.int32)

    near_first = near_field(
        near_ids(chosen[:early], 0), extended[:, :DIM], cols, early, near_count
    )
    theirs_first = lax.ppermute(near_first[:, columns:], "rhs", swap)
    first_half, second_half, _ = lax.optimization_barrier((first_half, second_half, near_first))

    parts = pl.pallas_call(
        functools.partial(far_kernel, 32),
        out_shape=jax.ShapeDtypeStruct((SIDE, pairs, columns, 2 * rank), F32),
        in_specs=[smem] + [anywhere] * 2 + [vmem],
        out_specs=vmem,
        scratch_shapes=[
            pltpu.VMEM((2 * SIDE * SIDE * rows_each, 2 * DIM, 2 * rank), BF16),
            pltpu.VMEM((SIDE * (2 * pairs + 1), columns, rank), F32),
            pltpu.SemaphoreType.DMA((2,)),
        ],
        compiler_params=params,
        cost_estimate=pl.CostEstimate(
            flops=3 * 10**10, bytes_accessed=10 * 2**20, transcendentals=0
        ),
        name="far",
    )(lists, first_half, second_half, skels)
    total = lax.psum_scatter(
        parts, "leaf", scatter_dimension=0, axis_index_groups=lines(2), tiled=True
    )[0]

    late_ids, _ = lax.optimization_barrier((near_ids(chosen[early:], early), parts))
    near_last = near_field(late_ids, extended[:, :DIM], cols, half - early, near_count)
    theirs_last = lax.ppermute(near_last[:, columns:], "rhs", swap)
    near_half = jnp.concatenate([near_first, near_last], axis=0)
    near_theirs = jnp.concatenate([theirs_first, theirs_last], axis=0)

    limits = jnp.concatenate([counts, core[None]]).astype(jnp.int32)
    return pl.pallas_call(
        final_kernel,
        out_shape=jax.ShapeDtypeStruct((leaf_dev, columns, leaf_size), F32),
        in_specs=[smem] + [vmem] * 5,
        out_specs=vmem,
        compiler_params=params,
        name="final",
    )(limits, transfer, leaf_basis, near_half, near_theirs, total)


def solution(mesh):
    return jax.shard_map(
        body,
        mesh=mesh,
        in_specs=(
            P("leaf", None, None),
            P("leaf", "rhs", None),
            P("leaf"),
            P("leaf", None, None),
            P("leaf", None, None),
            P("leaf", None, None),
            P("leaf", None, None),
            P("leaf", None),
            P("leaf", None),
            P("leaf", None),
            P("leaf", None),
            P("leaf", None),
        ),
        out_specs=P("leaf", "rhs", None),
        check_vma=False,
    )
```

```python
import functools
import math

import jax
import jax.numpy as jnp
from jax import lax
from jax.experimental import pallas as pl
from jax.experimental.pallas import tpu as pltpu
from jax.sharding import PartitionSpec as P

DIM = 8
HALO = 4


SQRT_THREE = 1.7320508075688772
LENGTH_SCALE = 1.5


RATE = SQRT_THREE / LENGTH_SCALE
RATE_TWO = RATE * math.log2(math.e)
BF16 = jnp.bfloat16
F32 = jnp.float32


def matern_of_square(square):
    square = jnp.maximum(square, 1e-30)
    radius = square * lax.rsqrt(square)
    return ((1.0 + RATE * radius) * jnp.exp2(-RATE_TWO * radius)).astype(BF16)


def norm_rows(coords):
    norm = jnp.sum(coords * coords, axis=0, keepdims=True)
    high = norm.astype(BF16).astype(F32)
    middle = (norm - high).astype(BF16).astype(F32)
    low = norm - high - middle
    row = lax.broadcasted_iota(jnp.int32, coords.shape, 0)
    return row, high, middle, low


def source_form(coords):
    row, high, middle, low = norm_rows(coords)
    tail = jnp.where(row == 0, high, jnp.where(row == 1, middle, jnp.where(row == 2, low, 1.0)))
    return jnp.concatenate([coords, jnp.where(row < 6, tail, 0.0)], axis=0)


def target_form(coords):
    row, high, middle, low = norm_rows(coords)
    tail = jnp.where(row == 3, high, jnp.where(row == 4, middle, jnp.where(row == 5, low, 1.0)))
    return jnp.concatenate([-2.0 * coords, jnp.where(row < 6, tail, 0.0)], axis=0)


def near_kernel(near, leaves, ids, pts, cols, out, rows, mine, even, odd):
    half = out.shape[0]
    size = pts.shape[2]
    base = ids[half * near]

    group = 8

    def stage(k, carry):
        forms = [source_form(pts[k * group + n].astype(F32)) for n in range(group)]
        turned = [form.T.astype(BF16) for form in forms]
        for n in range(group):
            rows[k * group + n] = turned[n]
        return carry

    lax.fori_loop(0, leaves // group, stage, 0)

    def stage_target(k, carry):
        forms = [target_form(pts[base + k * group + n].astype(F32)) for n in range(group)]
        for n in range(group):
            mine[k * group + n] = forms[n].astype(BF16)
        return carry

    lax.fori_loop(0, half // group, stage_target, 0)

    def values(i, j, store):
        square = jnp.dot(rows[ids[i * near + j]], mine[i], preferred_element_type=F32)
        store[size * j : size * (j + 1), :] = matern_of_square(square)

    def phase(current, previous, store, ready):
        total = jnp.zeros((cols.shape[1], size), F32)
        for j in range(near):
            values(current, j, store)
            total = total + jnp.dot(
                cols[ids[previous * near + j]],
                ready[size * j : size * (j + 1), :],
                preferred_element_type=F32,
            )
        out[previous] = total

    for j in range(near):
        values(0, j, even)

    def step(k, carry):
        phase(2 * k + 1, 2 * k, odd, even)
        phase(jnp.minimum(2 * k + 2, half - 1), 2 * k + 1, even, odd)
        return carry

    lax.fori_loop(0, half // 2, step, 0)


def near_field(ids, pts, cols, half, near):
    leaves, _, size = pts.shape
    vmem = pl.BlockSpec(memory_space=pltpu.VMEM)
    return pl.pallas_call(
        functools.partial(near_kernel, near, leaves),
        out_shape=jax.ShapeDtypeStruct((half, cols.shape[1], size), F32),
        in_specs=[pl.BlockSpec(memory_space=pltpu.SMEM), vmem, vmem],
        out_specs=vmem,
        scratch_shapes=[
            pltpu.VMEM((leaves, size, 2 * DIM), BF16),
            pltpu.VMEM((half, 2 * DIM, size), BF16),
            pltpu.VMEM((near * size, size), BF16),
            pltpu.VMEM((near * size, size), BF16),
        ],
        compiler_params=pltpu.CompilerParams(vmem_limit_bytes=40 * 2**20),
        cost_estimate=pl.CostEstimate(
            flops=half * near * size * size * 64, bytes_accessed=4 * 2**20, transcendentals=0
        ),
        name="near",
    )(ids, pts, cols)


def with_halo(cells, sides, width):
    for axis, dim in sides:
        count = lax.axis_size(axis)
        ends = count - 1
        head = lax.slice_in_dim(cells, 0, width, axis=dim)
        tail = lax.slice_in_dim(cells, cells.shape[dim] - width, cells.shape[dim], axis=dim)
        cells = jnp.concatenate(
            [
                lax.ppermute(tail, axis, [(i, (i + 1) % count) for i in range(ends)]),
                cells,
                lax.ppermute(head, axis, [((i + 1) % count, i) for i in range(ends)]),
            ],
            axis=dim,
        )
    return cells


SIDE = 4


def coef_kernel(values, basis, transfer, leaf_skel, upper_skel, table):
    pairs = leaf_skel.shape[0] // 2
    step_pairs = 8

    def step(i, carry):
        first = i * step_pairs
        coefs = [
            lax.dot_general(
                values[2 * first + n],
                basis[2 * first + n],
                (((1,), (1,)), ((), ())),
                preferred_element_type=F32,
            )
            for n in range(2 * step_pairs)
        ]
        coefs = [jnp.concatenate(coefs[2 * n : 2 * n + 2], axis=1) for n in range(step_pairs)]
        upper = []
        for n in range(step_pairs):
            p = first + n
            stacked = jnp.concatenate([transfer[2 * p], transfer[2 * p + 1]], axis=0)
            upper.append(jnp.dot(coefs[n].astype(BF16), stacked, preferred_element_type=F32))
        for n in range(step_pairs):
            p = first + n
            skel = [leaf_skel[2 * p + k].astype(F32) for k in range(2)]
            table[p] = jnp.concatenate(
                [jnp.concatenate(skel, axis=1), coefs[n]], axis=0
            ).astype(BF16)
        for n in range(step_pairs // 2):
            p = i * (step_pairs // 2) + n
            skel = [upper_skel[2 * p + k].astype(F32) for k in range(2)]
            coef = jnp.concatenate(upper[2 * n : 2 * n + 2], axis=1)
            table[pairs + p] = jnp.concatenate(
                [jnp.concatenate(skel, axis=1), coef], axis=0
            ).astype(BF16)
        return carry

    lax.fori_loop(0, pairs // step_pairs, step, 0)


def far_kernel(units, *refs):
    lists, (first_half, *rest), skels = refs[:4], refs[4:9], refs[9:13]
    outs, table, sums, sems = refs[13:]
    block = first_half.shape[0]
    copies = [
        pltpu.make_async_copy(first_half, table.at[pl.ds(0, block)], sems.at[0]),
    ]
    for n, piece in enumerate(rest):
        size = piece.shape[0]
        place = table.at[pl.ds(block + n * size, size)]
        copies.append(pltpu.make_async_copy(piece, place, sems.at[n + 1]))
    for copy in copies:
        copy.start()
    targets = 2 * skels[0].shape[0]
    rank = skels[0].shape[2] // 2
    lane = lax.broadcasted_iota(jnp.int32, (DIM, 2 * rank), 1)
    low = lane < rank

    def clear(i, carry):
        for n in range(4):
            sums[i * 4 + n] = jnp.zeros(sums.shape[1:], F32)
        return carry

    lax.fori_loop(0, sums.shape[0] // 4, clear, 0)
    for copy in copies:
        copy.wait()

    def turned(array):
        return jnp.concatenate([array[:, rank:], array[:, :rank]], axis=1)

    for r in range(SIDE):
        listed, skel, first = lists[r], skels[r], r * (targets + 1)

        def step(i, carry):
            where, squares, weights = [], [], []
            for quad in range(units // 4):
                left, right, coefs = [], [], []
                for n in range(4):
                    entry = listed[i * units + quad * 4 + n]
                    target = entry >> 12
                    row = (entry >> 1) & 2047
                    source = table[row].astype(F32)
                    swap = (entry & 1) != (n % 2)
                    source = jnp.where(swap, turned(source), source)
                    keep = low if n % 2 == 0 else jnp.logical_not(low)
                    form = jnp.where(
                        jnp.concatenate([keep, keep], axis=0), source_form(source[:DIM]), 0.0
                    )
                    coef = jnp.where(keep, source[DIM:], 0.0)
                    blank = jnp.zeros_like(form)
                    empty = jnp.zeros_like(coef)
                    wide = [form, blank] if n < 2 else [blank, form]
                    right.append(jnp.concatenate(wide, axis=1))
                    wide = [coef, empty] if n < 2 else [empty, coef]
                    coefs.append(jnp.concatenate(wide, axis=1))
                    pair = skel[jnp.minimum(target, targets - 1) >> 1].astype(F32)
                    pair = jnp.where((target & 1) == 1, turned(pair), pair)
                    left.append(target_form(pair))
                    where.append(first + target)
                left = jnp.concatenate(left, axis=0)[:, :rank].astype(BF16)
                right = jnp.concatenate(right, axis=0).astype(BF16)
                weights.append(jnp.concatenate(coefs, axis=0).astype(BF16))
                squares.append(
                    lax.dot_general(
                        left, right, (((0,), (0,)), ((), ())), preferred_element_type=F32
                    )
                )
            kernels = [matern_of_square(square) for square in squares]
            fields = [
                lax.dot_general(
                    weight, kernel, (((1,), (1,)), ((), ())), preferred_element_type=F32
                )
                for weight, kernel in zip(weights, kernels)
            ]
            for n in range(units):
                at = DIM * (n % 4)
                sums[where[n]] += fields[n // 4][at : at + DIM]
            return carry

        count = listed[listed.shape[0] - 128]
        origin = listed[listed.shape[0] - 127]
        lax.fori_loop(0, (count + units - 1) // units, step, 0)

        def pack(k, carry):
            for n in range(8):
                p = k * 8 + n
                both = [sums[first + 2 * p], sums[first + 2 * p + 1]]
                outs[origin, p] = jnp.concatenate(both, axis=1)
            return carry

        lax.fori_loop(0, targets // 16, pack, 0)


def final_kernel(counts, transfer, basis, near_mine, near_theirs, total, out):
    leaves = out.shape[0]
    half = leaves // 2
    rank = transfer.shape[1]
    core = counts[leaves]
    lane = lax.broadcasted_iota(jnp.int32, out.shape[1:], 1)
    group = 16

    def step(i, carry):
        first = i * group
        upper = [total[half + first // 4 + n].astype(BF16) for n in range(group // 4)]
        down = [
            lax.dot_general(
                upper[n // 4][:, (n // 2 % 2) * rank : (n // 2 % 2 + 1) * rank],
                transfer[first + n],
                (((1,), (1,)), ((), ())),
                preferred_element_type=F32,
            )
            for n in range(group)
        ]
        pairs = [total[first // 2 + n] for n in range(group // 2)]
        field = [
            (pairs[n // 2][:, (n % 2) * rank : (n % 2 + 1) * rank] + down[n]).astype(BF16)
            for n in range(group)
        ]
        result = [
            jnp.dot(field[n], basis[first + n], preferred_element_type=F32) for n in range(group)
        ]
        owner = first // half
        inner = first - owner * half
        for n in range(group):
            near = jnp.where(
                owner == core, near_mine[inner + n][: out.shape[1]], near_theirs[inner + n]
            )
            out[first + n] = jnp.where(lane < counts[first + n], result[n] + near, 0.0)
        return carry

    lax.fori_loop(0, leaves // group, step, 0)


def lines(axis):
    stride = (SIDE * SIDE, SIDE, 1)[axis]
    starts = [i for i in range(SIDE**3) if i // stride % SIDE == 0]
    return [[start + stride * k for k in range(SIDE)] for start in starts]


def line_gather(block, axis):
    return lax.all_gather(block, "leaf", axis_index_groups=lines(axis), tiled=True)


def line_shift(block, axis, by):
    pairs = [
        (line[(k + by) % SIDE], line[k]) for line in lines(axis) for k in range(SIDE)
    ]
    return lax.ppermute(block, "leaf", pairs)


def line_shifts(block, axis):
    return [block] + [line_shift(block, axis, by) for by in range(1, SIDE)]


def unit_lists(leaf_owner, leaf_local, upper_owner, upper_local, rows_each, capacity):
    me = lax.axis_index("leaf")
    leaves = leaf_owner.shape[0]
    parents = upper_owner.shape[0]

    def coded(owner, local, first_pair, first_target):
        x = owner // (SIDE * SIDE)
        x_ahead = (x - me // (SIDE * SIDE)) % SIDE
        y_ahead = (owner // SIDE - me // SIDE) % SIDE
        pair = first_pair + local // 2
        row = jnp.where(
            pair < rows_each,
            (x * SIDE + y_ahead) * rows_each + pair,
            (SIDE * SIDE + y_ahead * SIDE + x_ahead - 1) * rows_each + pair,
        )
        target = first_target + lax.broadcasted_iota(jnp.int32, owner.shape, 0)
        return (owner % SIDE << 20) | (target << 12) | (row << 1) | (local & 1)

    code = jnp.concatenate(
        [
            coded(leaf_owner, leaf_local, 0, 0),
            coded(upper_owner, upper_local, leaves // 2, leaves),
        ],
        axis=0,
    ).reshape(-1)
    hits = (code[:, None] >> 20 == jnp.arange(SIDE, dtype=jnp.int32)[None, :]).astype(BF16)
    code = code & (2**20 - 1)
    number = code.shape[0]
    order = jnp.arange(number, dtype=jnp.int32)
    before = (order[None, :] < order[:, None]).astype(BF16)
    rank = jnp.sum(jnp.dot(before, hits, preferred_element_type=F32) * hits.astype(F32), axis=1)
    spot = (rank.astype(jnp.int32)[:, None] == jnp.arange(capacity, dtype=jnp.int32)[None, :]).astype(
        BF16
    )
    digits = jnp.stack(
        [(code & 127), ((code >> 7) & 127), (code >> 14), jnp.ones_like(code)], axis=0
    ).astype(BF16)
    weights = (hits.T[:, None, :] * digits[None]).reshape(SIDE * 4, number)
    found = jnp.dot(weights, spot, preferred_element_type=F32).astype(jnp.int32)
    found = found.reshape(SIDE, 4, capacity)
    codes = found[:, 0] + (found[:, 1] << 7) + (found[:, 2] << 14)
    codes = codes + jnp.where(found[:, 3] == 0, (leaves + parents) << 12, 0)
    counts = jnp.sum(found[:, 3], axis=1)
    tail = jnp.where(jnp.arange(128)[None, :] == 0, counts[:, None], me % SIDE)
    return jnp.concatenate([codes, tail], axis=1)


def body(
    points,
    values,
    counts,
    leaf_basis,
    transfer,
    leaf_skeleton,
    upper_skeleton,
    near_list,
    far_owner,
    far_local,
    upper_owner,
    upper_local,
):
    leaf_dev = points.shape[0]
    leaf_size = points.shape[2]
    columns = values.shape[1]
    rank = leaf_basis.shape[1]
    near_count = near_list.shape[1]
    half = leaf_dev // 2
    pairs = leaf_dev // 2 + leaf_dev // 4
    rows_each = pairs // 2
    capacity = leaf_dev * far_owner.shape[1] * 3 // 4
    me = lax.axis_index("leaf")
    core = lax.axis_index("rhs")
    swap = [(0, 1), (1, 0)]
    vmem = pl.BlockSpec(memory_space=pltpu.VMEM)
    smem = pl.BlockSpec(memory_space=pltpu.SMEM)
    anywhere = pl.BlockSpec(memory_space=pl.ANY)
    params = pltpu.CompilerParams(vmem_limit_bytes=40 * 2**20)

    point_live = lax.broadcasted_iota(jnp.int32, (leaf_dev, leaf_size), 1) < counts[:, None]
    masked = jnp.where(point_live[:, None, :], values, jnp.zeros_like(values))
    table = pl.pallas_call(
        coef_kernel,
        out_shape=jax.ShapeDtypeStruct((pairs, 2 * DIM, 2 * rank), BF16),
        in_specs=[vmem] * 5,
        out_specs=vmem,
        compiler_params=params,
        cost_estimate=pl.CostEstimate(flops=10**8, bytes_accessed=6 * 2**20, transcendentals=0),
        name="coef",
    )(masked, leaf_basis, transfer, leaf_skeleton, upper_skeleton)
    first_half = line_gather(jnp.concatenate(line_shifts(table[:rows_each], 1), axis=0), 0)
    second_half = line_shifts(jnp.concatenate(line_shifts(table[rows_each:], 0), axis=0), 1)
    skels = line_shifts(table[:, :DIM], 2)
    lists = unit_lists(far_owner, far_local, upper_owner, upper_local, rows_each, capacity)
    all_lists = [lists[me % SIDE]]
    for r in range(1, SIDE):
        all_lists.append(line_shift(lists[(me - r) % SIDE], 2, r))

    bundle = jnp.concatenate([points, masked], axis=1)
    extended = with_halo(bundle, (("leaf", 0),), HALO)
    own = extended[:, DIM:]
    cols = jnp.concatenate([own, lax.ppermute(own, "rhs", swap)], axis=1)
    first_leaf = me * leaf_dev - HALO
    chosen = lax.dynamic_slice_in_dim(near_list - first_leaf, core * half, half, axis=0)
    start = core * half + HALO
    early = half * 5 // 8

    def near_ids(rows, offset):
        return jnp.concatenate([rows.reshape(-1), (start + offset)[None]]).astype(jnp.int32)

    near_first = near_field(
        near_ids(chosen[:early], 0), extended[:, :DIM], cols, early, near_count
    )
    theirs_first = lax.ppermute(near_first[:, columns:], "rhs", swap)
    first_half, _ = lax.optimization_barrier((first_half, near_first))

    parts = pl.pallas_call(
        functools.partial(far_kernel, 32),
        out_shape=jax.ShapeDtypeStruct((SIDE, pairs, columns, 2 * rank), F32),
        in_specs=[smem] * 4 + [anywhere] * 5 + [vmem] * 4,
        out_specs=vmem,
        scratch_shapes=[
            pltpu.VMEM((2 * SIDE * SIDE * rows_each, 2 * DIM, 2 * rank), BF16),
            pltpu.VMEM((SIDE * (2 * pairs + 1), columns, rank), F32),
            pltpu.SemaphoreType.DMA((5,)),
        ],
        compiler_params=params,
        cost_estimate=pl.CostEstimate(
            flops=3 * 10**10, bytes_accessed=10 * 2**20, transcendentals=0
        ),
        name="far",
    )(*all_lists, first_half, *second_half, *skels)
    total = lax.psum_scatter(
        parts, "leaf", scatter_dimension=0, axis_index_groups=lines(2), tiled=True
    )[0]

    late_ids, _ = lax.optimization_barrier((near_ids(chosen[early:], early), parts))
    near_last = near_field(late_ids, extended[:, :DIM], cols, half - early, near_count)
    theirs_last = lax.ppermute(near_last[:, columns:], "rhs", swap)
    near_half = jnp.concatenate([near_first, near_last], axis=0)
    near_theirs = jnp.concatenate([theirs_first, theirs_last], axis=0)

    limits = jnp.concatenate([counts, core[None]]).astype(jnp.int32)
    return pl.pallas_call(
        final_kernel,
        out_shape=jax.ShapeDtypeStruct((leaf_dev, columns, leaf_size), F32),
        in_specs=[smem] + [vmem] * 5,
        out_specs=vmem,
        compiler_params=params,
        name="final",
    )(limits, transfer, leaf_basis, near_half, near_theirs, total)


def solution(mesh):
    return jax.shard_map(
        body,
        mesh=mesh,
        in_specs=(
            P("leaf", None, None),
            P("leaf", "rhs", None),
            P("leaf"),
            P("leaf", None, None),
            P("leaf", None, None),
            P("leaf", None, None),
            P("leaf", None, None),
            P("leaf", None),
            P("leaf", None),
            P("leaf", None),
            P("leaf", None),
            P("leaf", None),
        ),
        out_specs=P("leaf", "rhs", None),
        check_vma=False,
    )
```

```python
import functools
import math

import jax
import jax.numpy as jnp
from jax import lax
from jax.experimental import pallas as pl
from jax.experimental.pallas import tpu as pltpu
from jax.sharding import PartitionSpec as P

DIM = 8
HALO = 4


SQRT_THREE = 1.7320508075688772
LENGTH_SCALE = 1.5


RATE = SQRT_THREE / LENGTH_SCALE
RATE_TWO = RATE * math.log2(math.e)
BF16 = jnp.bfloat16
F32 = jnp.float32


def matern_of_square(square):
    square = jnp.maximum(square, 1e-30)
    radius = square * lax.rsqrt(square)
    return ((1.0 + RATE * radius) * jnp.exp2(-RATE_TWO * radius)).astype(BF16)


def norm_rows(coords):
    norm = jnp.sum(coords * coords, axis=0, keepdims=True)
    high = norm.astype(BF16).astype(F32)
    middle = (norm - high).astype(BF16).astype(F32)
    low = norm - high - middle
    row = lax.broadcasted_iota(jnp.int32, coords.shape, 0)
    return row, high, middle, low


def source_form(coords):
    row, high, middle, low = norm_rows(coords)
    tail = jnp.where(row == 0, high, jnp.where(row == 1, middle, jnp.where(row == 2, low, 1.0)))
    return jnp.concatenate([coords, jnp.where(row < 6, tail, 0.0)], axis=0)


def target_form(coords):
    row, high, middle, low = norm_rows(coords)
    tail = jnp.where(row == 3, high, jnp.where(row == 4, middle, jnp.where(row == 5, low, 1.0)))
    return jnp.concatenate([-2.0 * coords, jnp.where(row < 6, tail, 0.0)], axis=0)


def near_kernel(near, leaves, ids, pts, cols, out, rows, mine, even, odd):
    half = out.shape[0]
    size = pts.shape[2]
    base = ids[half * near]

    group = 8

    def stage(k, carry):
        forms = [source_form(pts[k * group + n].astype(F32)) for n in range(group)]
        turned = [form.T.astype(BF16) for form in forms]
        for n in range(group):
            rows[k * group + n] = turned[n]
        return carry

    lax.fori_loop(0, leaves // group, stage, 0)

    def stage_target(k, carry):
        forms = [target_form(pts[base + k * group + n].astype(F32)) for n in range(group)]
        for n in range(group):
            mine[k * group + n] = forms[n].astype(BF16)
        return carry

    lax.fori_loop(0, half // group, stage_target, 0)

    def values(i, j, store):
        square = jnp.dot(rows[ids[i * near + j]], mine[i], preferred_element_type=F32)
        store[size * j : size * (j + 1), :] = matern_of_square(square)

    def phase(current, previous, store, ready):
        total = jnp.zeros((cols.shape[1], size), F32)
        for j in range(near):
            values(current, j, store)
            total = total + jnp.dot(
                cols[ids[previous * near + j]],
                ready[size * j : size * (j + 1), :],
                preferred_element_type=F32,
            )
        out[previous] = total

    for j in range(near):
        values(0, j, even)

    def step(k, carry):
        phase(2 * k + 1, 2 * k, odd, even)
        phase(jnp.minimum(2 * k + 2, half - 1), 2 * k + 1, even, odd)
        return carry

    lax.fori_loop(0, half // 2, step, 0)


def near_field(ids, pts, cols, half, near):
    leaves, _, size = pts.shape
    vmem = pl.BlockSpec(memory_space=pltpu.VMEM)
    return pl.pallas_call(
        functools.partial(near_kernel, near, leaves),
        out_shape=jax.ShapeDtypeStruct((half, cols.shape[1], size), F32),
        in_specs=[pl.BlockSpec(memory_space=pltpu.SMEM), vmem, vmem],
        out_specs=vmem,
        scratch_shapes=[
            pltpu.VMEM((leaves, size, 2 * DIM), BF16),
            pltpu.VMEM((half, 2 * DIM, size), BF16),
            pltpu.VMEM((near * size, size), BF16),
            pltpu.VMEM((near * size, size), BF16),
        ],
        compiler_params=pltpu.CompilerParams(vmem_limit_bytes=40 * 2**20),
        cost_estimate=pl.CostEstimate(
            flops=half * near * size * size * 64, bytes_accessed=4 * 2**20, transcendentals=0
        ),
        name="near",
    )(ids, pts, cols)


def with_halo(cells, sides, width):
    for axis, dim in sides:
        count = lax.axis_size(axis)
        ends = count - 1
        head = lax.slice_in_dim(cells, 0, width, axis=dim)
        tail = lax.slice_in_dim(cells, cells.shape[dim] - width, cells.shape[dim], axis=dim)
        cells = jnp.concatenate(
            [
                lax.ppermute(tail, axis, [(i, (i + 1) % count) for i in range(ends)]),
                cells,
                lax.ppermute(head, axis, [((i + 1) % count, i) for i in range(ends)]),
            ],
            axis=dim,
        )
    return cells


SIDE = 4


def coef_kernel(values, basis, transfer, leaf_skel, upper_skel, table):
    pairs = leaf_skel.shape[0] // 2
    step_pairs = 8

    def step(i, carry):
        first = i * step_pairs
        coefs = [
            lax.dot_general(
                values[2 * first + n],
                basis[2 * first + n],
                (((1,), (1,)), ((), ())),
                preferred_element_type=F32,
            )
            for n in range(2 * step_pairs)
        ]
        coefs = [jnp.concatenate(coefs[2 * n : 2 * n + 2], axis=1) for n in range(step_pairs)]
        upper = []
        for n in range(step_pairs):
            p = first + n
            stacked = jnp.concatenate([transfer[2 * p], transfer[2 * p + 1]], axis=0)
            upper.append(jnp.dot(coefs[n].astype(BF16), stacked, preferred_element_type=F32))
        for n in range(step_pairs):
            p = first + n
            skel = [leaf_skel[2 * p + k].astype(F32) for k in range(2)]
            table[p] = jnp.concatenate(
                [jnp.concatenate(skel, axis=1), coefs[n]], axis=0
            ).astype(BF16)
        for n in range(step_pairs // 2):
            p = i * (step_pairs // 2) + n
            skel = [upper_skel[2 * p + k].astype(F32) for k in range(2)]
            coef = jnp.concatenate(upper[2 * n : 2 * n + 2], axis=1)
            table[pairs + p] = jnp.concatenate(
                [jnp.concatenate(skel, axis=1), coef], axis=0
            ).astype(BF16)
        return carry

    lax.fori_loop(0, pairs // step_pairs, step, 0)


def far_kernel(units, *refs):
    lists, gathered, skels = refs[:4], refs[4], refs[5:9]
    outs, table, sums, sem = refs[9:]
    copy = pltpu.make_async_copy(gathered, table, sem)
    copy.start()
    targets = 2 * skels[0].shape[0]
    rank = skels[0].shape[2] // 2
    lane = lax.broadcasted_iota(jnp.int32, (DIM, 2 * rank), 1)
    low = lane < rank

    def clear(i, carry):
        for n in range(4):
            sums[i * 4 + n] = jnp.zeros(sums.shape[1:], F32)
        return carry

    lax.fori_loop(0, sums.shape[0] // 4, clear, 0)
    copy.wait()

    def turned(array):
        return jnp.concatenate([array[:, rank:], array[:, :rank]], axis=1)

    for r in range(SIDE):
        listed, skel, first = lists[r], skels[r], r * (targets + 1)

        def step(i, carry):
            where, squares, weights = [], [], []
            for quad in range(units // 4):
                left, right, coefs = [], [], []
                for n in range(4):
                    entry = listed[i * units + quad * 4 + n]
                    target = entry >> 12
                    row = (entry >> 1) & 2047
                    source = table[row].astype(F32)
                    swap = (entry & 1) != (n % 2)
                    source = jnp.where(swap, turned(source), source)
                    keep = low if n % 2 == 0 else jnp.logical_not(low)
                    form = jnp.where(
                        jnp.concatenate([keep, keep], axis=0), source_form(source[:DIM]), 0.0
                    )
                    coef = jnp.where(keep, source[DIM:], 0.0)
                    blank = jnp.zeros_like(form)
                    empty = jnp.zeros_like(coef)
                    wide = [form, blank] if n < 2 else [blank, form]
                    right.append(jnp.concatenate(wide, axis=1))
                    wide = [coef, empty] if n < 2 else [empty, coef]
                    coefs.append(jnp.concatenate(wide, axis=1))
                    pair = skel[jnp.minimum(target, targets - 1) >> 1].astype(F32)
                    pair = jnp.where((target & 1) == 1, turned(pair), pair)
                    left.append(target_form(pair))
                    where.append(first + target)
                left = jnp.concatenate(left, axis=0)[:, :rank].astype(BF16)
                right = jnp.concatenate(right, axis=0).astype(BF16)
                weights.append(jnp.concatenate(coefs, axis=0).astype(BF16))
                squares.append(
                    lax.dot_general(
                        left, right, (((0,), (0,)), ((), ())), preferred_element_type=F32
                    )
                )
            kernels = [matern_of_square(square) for square in squares]
            fields = [
                lax.dot_general(
                    weight, kernel, (((1,), (1,)), ((), ())), preferred_element_type=F32
                )
                for weight, kernel in zip(weights, kernels)
            ]
            for n in range(units):
                at = DIM * (n % 4)
                sums[where[n]] += fields[n // 4][at : at + DIM]
            return carry

        count = listed[listed.shape[0] - 128]
        origin = listed[listed.shape[0] - 127]
        lax.fori_loop(0, (count + units - 1) // units, step, 0)

        def pack(k, carry):
            for n in range(8):
                p = k * 8 + n
                both = [sums[first + 2 * p], sums[first + 2 * p + 1]]
                outs[origin, p] = jnp.concatenate(both, axis=1)
            return carry

        lax.fori_loop(0, targets // 16, pack, 0)


def final_kernel(counts, transfer, basis, near_mine, near_theirs, total, out):
    leaves = out.shape[0]
    half = leaves // 2
    rank = transfer.shape[1]
    core = counts[leaves]
    lane = lax.broadcasted_iota(jnp.int32, out.shape[1:], 1)
    group = 16

    def step(i, carry):
        first = i * group
        upper = [total[half + first // 4 + n].astype(BF16) for n in range(group // 4)]
        down = [
            lax.dot_general(
                upper[n // 4][:, (n // 2 % 2) * rank : (n // 2 % 2 + 1) * rank],
                transfer[first + n],
                (((1,), (1,)), ((), ())),
                preferred_element_type=F32,
            )
            for n in range(group)
        ]
        pairs = [total[first // 2 + n] for n in range(group // 2)]
        field = [
            (pairs[n // 2][:, (n % 2) * rank : (n % 2 + 1) * rank] + down[n]).astype(BF16)
            for n in range(group)
        ]
        result = [
            jnp.dot(field[n], basis[first + n], preferred_element_type=F32) for n in range(group)
        ]
        owner = first // half
        inner = first - owner * half
        for n in range(group):
            near = jnp.where(
                owner == core, near_mine[inner + n][: out.shape[1]], near_theirs[inner + n]
            )
            out[first + n] = jnp.where(lane < counts[first + n], result[n] + near, 0.0)
        return carry

    lax.fori_loop(0, leaves // group, step, 0)


def lines(axis):
    stride = (SIDE * SIDE, SIDE, 1)[axis]
    starts = [i for i in range(SIDE**3) if i // stride % SIDE == 0]
    return [[start + stride * k for k in range(SIDE)] for start in starts]


def plane_gather(block):
    groups = [[SIDE * k + z for k in range(SIDE * SIDE)] for z in range(SIDE)]
    return lax.all_gather(block, "leaf", axis_index_groups=groups, tiled=True)


def line_shift(block, axis, by):
    pairs = [
        (line[(k + by) % SIDE], line[k]) for line in lines(axis) for k in range(SIDE)
    ]
    return lax.ppermute(block, "leaf", pairs)


def line_shifts(block, axis):
    return [block] + [line_shift(block, axis, by) for by in range(1, SIDE)]


def list_kernel(codes, lists):
    count = codes.shape[1]
    capacity = lists.shape[1] - 128
    code = codes[0:1, :]
    row = lax.broadcasted_iota(jnp.int32, (8, count), 0)
    hits = jnp.where(row == code >> 20, 1.0, 0.0)
    code = jnp.broadcast_to(code & (2**20 - 1), (8, count))
    digits = [code & 127, (code >> 7) & 127, code >> 14]
    weights = [hits * digit.astype(F32) for digit in digits] + [hits]
    weights = jnp.concatenate(weights, axis=0).astype(BF16)
    chunk = 256
    ranks = jnp.zeros((8, count), F32)
    for n in range(count // chunk):
        before = lax.broadcasted_iota(jnp.int32, (chunk, count), 0) + n * chunk
        after = lax.broadcasted_iota(jnp.int32, (chunk, count), 1)
        ranks = ranks + jnp.dot(
            hits[:, n * chunk : (n + 1) * chunk].astype(BF16),
            jnp.where(before < after, 1.0, 0.0).astype(BF16),
            preferred_element_type=F32,
        )
    rank = jnp.sum(ranks * hits, axis=0, keepdims=True).astype(jnp.int32)
    parts = capacity // chunk
    for n in range(parts):
        place = lax.broadcasted_iota(jnp.int32, (chunk, count), 0) + n * chunk
        spot = jnp.where(place == rank, 1.0, 0.0).astype(BF16)
        found = lax.dot_general(
            weights, spot, (((1,), (1,)), ((), ())), preferred_element_type=F32
        ).astype(jnp.int32)
        joined = found[:8] + (found[8:16] << 7) + (found[16:24] << 14)
        dummy = codes[1:2, 0:chunk]
        lists[:, n * chunk : (n + 1) * chunk] = jnp.where(found[24:] == 0, dummy, joined)
    total = jnp.sum(hits, axis=1, keepdims=True).astype(jnp.int32)
    lane = lax.broadcasted_iota(jnp.int32, (8, 128), 1)
    lists[:, capacity:] = jnp.where(lane == 0, total, codes[2:3, 0:128])


def unit_lists(leaf_owner, leaf_local, upper_owner, upper_local, capacity):
    me = lax.axis_index("leaf")
    leaves = leaf_owner.shape[0]
    parents = upper_owner.shape[0]
    pairs = (leaves + parents) // 2

    def coded(owner, local, first_pair, first_target):
        row = owner // SIDE * pairs + first_pair + local // 2
        target = first_target + lax.broadcasted_iota(jnp.int32, owner.shape, 0)
        return (owner % SIDE << 20) | (target << 12) | (row << 1) | (local & 1)

    code = jnp.concatenate(
        [
            coded(leaf_owner, leaf_local, 0, 0),
            coded(upper_owner, upper_local, leaves // 2, leaves),
        ],
        axis=0,
    ).reshape(1, -1)
    kind = lax.broadcasted_iota(jnp.int32, (8, code.shape[1]), 0)
    dummy = (leaves + parents) << 12
    codes = jnp.where(kind == 0, code, jnp.where(kind == 1, dummy, me % SIDE))
    vmem = pl.BlockSpec(memory_space=pltpu.VMEM)
    return pl.pallas_call(
        list_kernel,
        out_shape=jax.ShapeDtypeStruct((8, capacity + 128), jnp.int32),
        in_specs=[vmem],
        out_specs=vmem,
        compiler_params=pltpu.CompilerParams(vmem_limit_bytes=40 * 2**20),
        cost_estimate=pl.CostEstimate(flops=10**8, bytes_accessed=10**5, transcendentals=0),
        name="lists",
    )(codes)


def body(
    points,
    values,
    counts,
    leaf_basis,
    transfer,
    leaf_skeleton,
    upper_skeleton,
    near_list,
    far_owner,
    far_local,
    upper_owner,
    upper_local,
):
    leaf_dev = points.shape[0]
    leaf_size = points.shape[2]
    columns = values.shape[1]
    rank = leaf_basis.shape[1]
    near_count = near_list.shape[1]
    half = leaf_dev // 2
    pairs = leaf_dev // 2 + leaf_dev // 4
    capacity = leaf_dev * far_owner.shape[1] * 3 // 4
    me = lax.axis_index("leaf")
    core = lax.axis_index("rhs")
    swap = [(0, 1), (1, 0)]
    vmem = pl.BlockSpec(memory_space=pltpu.VMEM)
    smem = pl.BlockSpec(memory_space=pltpu.SMEM)
    anywhere = pl.BlockSpec(memory_space=pl.ANY)
    params = pltpu.CompilerParams(vmem_limit_bytes=40 * 2**20)

    point_live = lax.broadcasted_iota(jnp.int32, (leaf_dev, leaf_size), 1) < counts[:, None]
    masked = jnp.where(point_live[:, None, :], values, jnp.zeros_like(values))
    table = pl.pallas_call(
        coef_kernel,
        out_shape=jax.ShapeDtypeStruct((pairs, 2 * DIM, 2 * rank), BF16),
        in_specs=[vmem] * 5,
        out_specs=vmem,
        compiler_params=params,
        cost_estimate=pl.CostEstimate(flops=10**8, bytes_accessed=6 * 2**20, transcendentals=0),
        name="coef",
    )(masked, leaf_basis, transfer, leaf_skeleton, upper_skeleton)
    gathered = plane_gather(table)
    skels = line_shifts(table[:, :DIM], 2)
    lists = unit_lists(far_owner, far_local, upper_owner, upper_local, capacity)
    all_lists = [lists[me % SIDE]]
    for r in range(1, SIDE):
        all_lists.append(line_shift(lists[(me - r) % SIDE], 2, r))

    bundle = jnp.concatenate([points, masked], axis=1)
    extended = with_halo(bundle, (("leaf", 0),), HALO)
    own = extended[:, DIM:]
    cols = jnp.concatenate([own, lax.ppermute(own, "rhs", swap)], axis=1)
    first_leaf = me * leaf_dev - HALO
    chosen = lax.dynamic_slice_in_dim(near_list - first_leaf, core * half, half, axis=0)
    start = core * half + HALO
    early = half * 5 // 8

    def near_ids(rows, offset):
        return jnp.concatenate([rows.reshape(-1), (start + offset)[None]]).astype(jnp.int32)

    near_first = near_field(
        near_ids(chosen[:early], 0), extended[:, :DIM], cols, early, near_count
    )
    theirs_first = lax.ppermute(near_first[:, columns:], "rhs", swap)
    gathered, _ = lax.optimization_barrier((gathered, near_first))

    parts = pl.pallas_call(
        functools.partial(far_kernel, 32),
        out_shape=jax.ShapeDtypeStruct((SIDE, pairs, columns, 2 * rank), F32),
        in_specs=[smem] * 4 + [anywhere] + [vmem] * 4,
        out_specs=vmem,
        scratch_shapes=[
            pltpu.VMEM((SIDE * SIDE * pairs, 2 * DIM, 2 * rank), BF16),
            pltpu.VMEM((SIDE * (2 * pairs + 1), columns, rank), F32),
            pltpu.SemaphoreType.DMA,
        ],
        compiler_params=params,
        cost_estimate=pl.CostEstimate(
            flops=3 * 10**10, bytes_accessed=10 * 2**20, transcendentals=0
        ),
        name="far",
    )(*all_lists, gathered, *skels)
    total = lax.psum_scatter(
        parts, "leaf", scatter_dimension=0, axis_index_groups=lines(2), tiled=True
    )[0]

    late_ids, _ = lax.optimization_barrier((near_ids(chosen[early:], early), parts))
    near_last = near_field(late_ids, extended[:, :DIM], cols, half - early, near_count)
    theirs_last = lax.ppermute(near_last[:, columns:], "rhs", swap)
    near_half = jnp.concatenate([near_first, near_last], axis=0)
    near_theirs = jnp.concatenate([theirs_first, theirs_last], axis=0)

    limits = jnp.concatenate([counts, core[None]]).astype(jnp.int32)
    return pl.pallas_call(
        final_kernel,
        out_shape=jax.ShapeDtypeStruct((leaf_dev, columns, leaf_size), F32),
        in_specs=[smem] + [vmem] * 5,
        out_specs=vmem,
        compiler_params=params,
        name="final",
    )(limits, transfer, leaf_basis, near_half, near_theirs, total)


def solution(mesh):
    return jax.shard_map(
        body,
        mesh=mesh,
        in_specs=(
            P("leaf", None, None),
            P("leaf", "rhs", None),
            P("leaf"),
            P("leaf", None, None),
            P("leaf", None, None),
            P("leaf", None, None),
            P("leaf", None, None),
            P("leaf", None),
            P("leaf", None),
            P("leaf", None),
            P("leaf", None),
            P("leaf", None),
        ),
        out_specs=P("leaf", "rhs", None),
        check_vma=False,
    )
```

```python
import functools
import math

import jax
import jax.numpy as jnp
from jax import lax
from jax.experimental import pallas as pl
from jax.experimental.pallas import tpu as pltpu
from jax.sharding import PartitionSpec as P

DIM = 8
HALO = 4


SQRT_THREE = 1.7320508075688772
LENGTH_SCALE = 1.5


RATE = SQRT_THREE / LENGTH_SCALE
RATE_TWO = RATE * math.log2(math.e)
BF16 = jnp.bfloat16
F32 = jnp.float32


def matern_of_square(square):
    square = jnp.maximum(square, 1e-30)
    radius = square * lax.rsqrt(square)
    return ((1.0 + RATE * radius) * jnp.exp2(-RATE_TWO * radius)).astype(BF16)


def norm_rows(coords):
    norm = jnp.sum(coords * coords, axis=0, keepdims=True)
    high = norm.astype(BF16).astype(F32)
    middle = (norm - high).astype(BF16).astype(F32)
    low = norm - high - middle
    row = lax.broadcasted_iota(jnp.int32, coords.shape, 0)
    return row, high, middle, low


def source_form(coords):
    row, high, middle, low = norm_rows(coords)
    tail = jnp.where(row == 0, high, jnp.where(row == 1, middle, jnp.where(row == 2, low, 1.0)))
    return jnp.concatenate([coords, jnp.where(row < 6, tail, 0.0)], axis=0)


def target_form(coords):
    row, high, middle, low = norm_rows(coords)
    tail = jnp.where(row == 3, high, jnp.where(row == 4, middle, jnp.where(row == 5, low, 1.0)))
    return jnp.concatenate([-2.0 * coords, jnp.where(row < 6, tail, 0.0)], axis=0)


def near_kernel(near, leaves, ids, pts, cols, out, rows, mine, even, odd):
    half = out.shape[0]
    size = pts.shape[2]
    base = ids[half * near]

    group = 8

    def stage(k, carry):
        forms = [source_form(pts[k * group + n].astype(F32)) for n in range(group)]
        turned = [form.T.astype(BF16) for form in forms]
        for n in range(group):
            rows[k * group + n] = turned[n]
        return carry

    lax.fori_loop(0, leaves // group, stage, 0)

    def stage_target(k, carry):
        forms = [target_form(pts[base + k * group + n].astype(F32)) for n in range(group)]
        for n in range(group):
            mine[k * group + n] = forms[n].astype(BF16)
        return carry

    lax.fori_loop(0, half // group, stage_target, 0)

    def values(i, j, store):
        square = jnp.dot(rows[ids[i * near + j]], mine[i], preferred_element_type=F32)
        store[size * j : size * (j + 1), :] = matern_of_square(square)

    def phase(current, previous, store, ready):
        total = jnp.zeros((cols.shape[1], size), F32)
        for j in range(near):
            values(current, j, store)
            total = total + jnp.dot(
                cols[ids[previous * near + j]],
                ready[size * j : size * (j + 1), :],
                preferred_element_type=F32,
            )
        out[previous] = total

    for j in range(near):
        values(0, j, even)

    def step(k, carry):
        phase(2 * k + 1, 2 * k, odd, even)
        phase(jnp.minimum(2 * k + 2, half - 1), 2 * k + 1, even, odd)
        return carry

    lax.fori_loop(0, half // 2, step, 0)


def near_field(ids, pts, cols, half, near):
    leaves, _, size = pts.shape
    vmem = pl.BlockSpec(memory_space=pltpu.VMEM)
    return pl.pallas_call(
        functools.partial(near_kernel, near, leaves),
        out_shape=jax.ShapeDtypeStruct((half, cols.shape[1], size), F32),
        in_specs=[pl.BlockSpec(memory_space=pltpu.SMEM), vmem, vmem],
        out_specs=vmem,
        scratch_shapes=[
            pltpu.VMEM((leaves, size, 2 * DIM), BF16),
            pltpu.VMEM((half, 2 * DIM, size), BF16),
            pltpu.VMEM((near * size, size), BF16),
            pltpu.VMEM((near * size, size), BF16),
        ],
        compiler_params=pltpu.CompilerParams(vmem_limit_bytes=40 * 2**20),
        cost_estimate=pl.CostEstimate(
            flops=half * near * size * size * 64, bytes_accessed=4 * 2**20, transcendentals=0
        ),
        name="near",
    )(ids, pts, cols)


def with_halo(cells, sides, width):
    for axis, dim in sides:
        count = lax.axis_size(axis)
        ends = count - 1
        head = lax.slice_in_dim(cells, 0, width, axis=dim)
        tail = lax.slice_in_dim(cells, cells.shape[dim] - width, cells.shape[dim], axis=dim)
        cells = jnp.concatenate(
            [
                lax.ppermute(tail, axis, [(i, (i + 1) % count) for i in range(ends)]),
                cells,
                lax.ppermute(head, axis, [((i + 1) % count, i) for i in range(ends)]),
            ],
            axis=dim,
        )
    return cells


SIDE = 4


def coef_kernel(values, basis, transfer, leaf_skel, upper_skel, table):
    pairs = leaf_skel.shape[0] // 2
    step_pairs = 8

    def step(i, carry):
        first = i * step_pairs
        coefs = [
            lax.dot_general(
                values[2 * first + n],
                basis[2 * first + n],
                (((1,), (1,)), ((), ())),
                preferred_element_type=F32,
            )
            for n in range(2 * step_pairs)
        ]
        coefs = [jnp.concatenate(coefs[2 * n : 2 * n + 2], axis=1) for n in range(step_pairs)]
        upper = []
        for n in range(step_pairs):
            p = first + n
            stacked = jnp.concatenate([transfer[2 * p], transfer[2 * p + 1]], axis=0)
            upper.append(jnp.dot(coefs[n].astype(BF16), stacked, preferred_element_type=F32))
        for n in range(step_pairs):
            p = first + n
            skel = [leaf_skel[2 * p + k].astype(F32) for k in range(2)]
            table[p] = jnp.concatenate(
                [jnp.concatenate(skel, axis=1), coefs[n]], axis=0
            ).astype(BF16)
        for n in range(step_pairs // 2):
            p = i * (step_pairs // 2) + n
            skel = [upper_skel[2 * p + k].astype(F32) for k in range(2)]
            coef = jnp.concatenate(upper[2 * n : 2 * n + 2], axis=1)
            table[pairs + p] = jnp.concatenate(
                [jnp.concatenate(skel, axis=1), coef], axis=0
            ).astype(BF16)
        return carry

    lax.fori_loop(0, pairs // step_pairs, step, 0)


def far_kernel(units, *refs):
    lists, table, skels = refs[:4], refs[4], refs[5:9]
    outs, sums = refs[9:]
    targets = 2 * skels[0].shape[0]
    rank = skels[0].shape[2] // 2
    lane = lax.broadcasted_iota(jnp.int32, (DIM, 2 * rank), 1)
    low = lane < rank
    wide = lax.broadcasted_iota(jnp.int32, (2 * DIM, 2 * rank), 1)
    low_wide = wide < rank
    keep_low = jnp.where(low_wide, 1.0, 0.0).astype(BF16)
    keep_high = jnp.where(low_wide, 0.0, 1.0).astype(BF16)
    blank = jnp.zeros((2 * DIM, 2 * rank), BF16)
    empty = jnp.zeros((DIM, 2 * rank), F32)

    def clear(i, carry):
        for n in range(4):
            sums[i * 4 + n] = jnp.zeros(sums.shape[1:], F32)
        return carry

    lax.fori_loop(0, sums.shape[0] // 4, clear, 0)

    def turned(array):
        return jnp.concatenate([array[:, rank:], array[:, :rank]], axis=1)

    for r in range(SIDE):
        listed, skel, first = lists[r], skels[r], r * (targets + 1)

        def step(i, carry):
            where, squares, weights = [], [], []
            for quad in range(units // 4):
                left, right, coefs = [], [], []
                for m in range(2):
                    sources, goals = [], []
                    for n in range(2):
                        entry = listed[i * units + quad * 4 + m * 2 + n]
                        target = entry >> 12
                        source = table[(entry >> 1) & 2047].astype(F32)
                        swap = (entry & 1) != n
                        sources.append(jnp.where(swap, turned(source), source))
                        goal = skel[jnp.minimum(target, targets - 1) >> 1].astype(F32)
                        swap = (target & 1) != n
                        goals.append(jnp.where(swap, turned(goal), goal))
                        where.append(first + target)
                    source = jnp.where(low_wide, sources[0], sources[1])
                    form = source_form(source[:DIM]).astype(BF16)
                    coef = source[DIM:]
                    for keep in (keep_low, keep_high):
                        pieces = [form * keep, blank] if m == 0 else [blank, form * keep]
                        right.append(jnp.concatenate(pieces, axis=1))
                    for piece in (jnp.where(low, coef, 0.0), jnp.where(low, 0.0, coef)):
                        pieces = [piece, empty] if m == 0 else [empty, piece]
                        coefs.append(jnp.concatenate(pieces, axis=1))
                    form = target_form(jnp.where(low, goals[0], goals[1]))
                    left += [form, turned(form)]
                left = jnp.concatenate(left, axis=0)[:, :rank].astype(BF16)
                right = jnp.concatenate(right, axis=0)
                weights.append(jnp.concatenate(coefs, axis=0).astype(BF16))
                squares.append(
                    lax.dot_general(
                        left, right, (((0,), (0,)), ((), ())), preferred_element_type=F32
                    )
                )
            kernels = [matern_of_square(square) for square in squares]
            fields = [
                lax.dot_general(
                    weight, kernel, (((1,), (1,)), ((), ())), preferred_element_type=F32
                )
                for weight, kernel in zip(weights, kernels)
            ]
            for n in range(units):
                at = DIM * (n % 4)
                sums[where[n]] += fields[n // 4][at : at + DIM]
            return carry

        count = listed[listed.shape[0] - 128]
        origin = listed[listed.shape[0] - 127]
        lax.fori_loop(0, (count + units - 1) // units, step, 0)

        def pack(k, carry):
            for n in range(8):
                p = k * 8 + n
                both = [sums[first + 2 * p], sums[first + 2 * p + 1]]
                outs[origin, p] = jnp.concatenate(both, axis=1)
            return carry

        lax.fori_loop(0, targets // 16, pack, 0)


def final_kernel(counts, transfer, basis, near_mine, near_theirs, total, out):
    leaves = out.shape[0]
    half = leaves // 2
    rank = transfer.shape[1]
    core = counts[leaves]
    lane = lax.broadcasted_iota(jnp.int32, out.shape[1:], 1)
    group = 16

    def step(i, carry):
        first = i * group
        upper = [total[half + first // 4 + n].astype(BF16) for n in range(group // 4)]
        down = [
            lax.dot_general(
                upper[n // 4][:, (n // 2 % 2) * rank : (n // 2 % 2 + 1) * rank],
                transfer[first + n],
                (((1,), (1,)), ((), ())),
                preferred_element_type=F32,
            )
            for n in range(group)
        ]
        pairs = [total[first // 2 + n] for n in range(group // 2)]
        field = [
            (pairs[n // 2][:, (n % 2) * rank : (n % 2 + 1) * rank] + down[n]).astype(BF16)
            for n in range(group)
        ]
        result = [
            jnp.dot(field[n], basis[first + n], preferred_element_type=F32) for n in range(group)
        ]
        owner = first // half
        inner = first - owner * half
        for n in range(group):
            near = jnp.where(
                owner == core, near_mine[inner + n][: out.shape[1]], near_theirs[inner + n]
            )
            out[first + n] = jnp.where(lane < counts[first + n], result[n] + near, 0.0)
        return carry

    lax.fori_loop(0, leaves // group, step, 0)


def lines(axis):
    stride = (SIDE * SIDE, SIDE, 1)[axis]
    starts = [i for i in range(SIDE**3) if i // stride % SIDE == 0]
    return [[start + stride * k for k in range(SIDE)] for start in starts]


def plane_gather(block):
    groups = [[SIDE * k + z for k in range(SIDE * SIDE)] for z in range(SIDE)]
    return lax.all_gather(block, "leaf", axis_index_groups=groups, tiled=True)


def line_shift(block, axis, by):
    pairs = [
        (line[(k + by) % SIDE], line[k]) for line in lines(axis) for k in range(SIDE)
    ]
    return lax.ppermute(block, "leaf", pairs)


def line_shifts(block, axis):
    return [block] + [line_shift(block, axis, by) for by in range(1, SIDE)]


def list_kernel(codes, lists):
    count = codes.shape[1]
    capacity = lists.shape[1] - 128
    code = codes[0:1, :]
    row = lax.broadcasted_iota(jnp.int32, (8, count), 0)
    hits = jnp.where(row == code >> 20, 1.0, 0.0)
    code = jnp.broadcast_to(code & (2**20 - 1), (8, count))
    digits = [code & 127, (code >> 7) & 127, code >> 14]
    weights = [hits * digit.astype(F32) for digit in digits] + [hits]
    weights = jnp.concatenate(weights, axis=0).astype(BF16)
    chunk = 256
    ranks = jnp.zeros((8, count), F32)
    for n in range(count // chunk):
        before = lax.broadcasted_iota(jnp.int32, (chunk, count), 0) + n * chunk
        after = lax.broadcasted_iota(jnp.int32, (chunk, count), 1)
        ranks = ranks + jnp.dot(
            hits[:, n * chunk : (n + 1) * chunk].astype(BF16),
            jnp.where(before < after, 1.0, 0.0).astype(BF16),
            preferred_element_type=F32,
        )
    rank = jnp.sum(ranks * hits, axis=0, keepdims=True).astype(jnp.int32)
    parts = capacity // chunk
    for n in range(parts):
        place = lax.broadcasted_iota(jnp.int32, (chunk, count), 0) + n * chunk
        spot = jnp.where(place == rank, 1.0, 0.0).astype(BF16)
        found = lax.dot_general(
            weights, spot, (((1,), (1,)), ((), ())), preferred_element_type=F32
        ).astype(jnp.int32)
        joined = found[:8] + (found[8:16] << 7) + (found[16:24] << 14)
        dummy = codes[1:2, 0:chunk]
        lists[:, n * chunk : (n + 1) * chunk] = jnp.where(found[24:] == 0, dummy, joined)
    total = jnp.sum(hits, axis=1, keepdims=True).astype(jnp.int32)
    lane = lax.broadcasted_iota(jnp.int32, (8, 128), 1)
    lists[:, capacity:] = jnp.where(lane == 0, total, codes[2:3, 0:128])


def unit_lists(leaf_owner, leaf_local, upper_owner, upper_local, capacity):
    me = lax.axis_index("leaf")
    leaves = leaf_owner.shape[0]
    parents = upper_owner.shape[0]
    pairs = (leaves + parents) // 2

    def coded(owner, local, first_pair, first_target):
        row = owner // SIDE * pairs + first_pair + local // 2
        target = first_target + lax.broadcasted_iota(jnp.int32, owner.shape, 0)
        return (owner % SIDE << 20) | (target << 12) | (row << 1) | (local & 1)

    code = jnp.concatenate(
        [
            coded(leaf_owner, leaf_local, 0, 0),
            coded(upper_owner, upper_local, leaves // 2, leaves),
        ],
        axis=0,
    ).reshape(1, -1)
    kind = lax.broadcasted_iota(jnp.int32, (8, code.shape[1]), 0)
    dummy = (leaves + parents) << 12
    codes = jnp.where(kind == 0, code, jnp.where(kind == 1, dummy, me % SIDE))
    vmem = pl.BlockSpec(memory_space=pltpu.VMEM)
    return pl.pallas_call(
        list_kernel,
        out_shape=jax.ShapeDtypeStruct((8, capacity + 128), jnp.int32),
        in_specs=[vmem],
        out_specs=vmem,
        compiler_params=pltpu.CompilerParams(vmem_limit_bytes=40 * 2**20),
        cost_estimate=pl.CostEstimate(flops=10**8, bytes_accessed=10**5, transcendentals=0),
        name="lists",
    )(codes)


def body(
    points,
    values,
    counts,
    leaf_basis,
    transfer,
    leaf_skeleton,
    upper_skeleton,
    near_list,
    far_owner,
    far_local,
    upper_owner,
    upper_local,
):
    leaf_dev = points.shape[0]
    leaf_size = points.shape[2]
    columns = values.shape[1]
    rank = leaf_basis.shape[1]
    near_count = near_list.shape[1]
    half = leaf_dev // 2
    pairs = leaf_dev // 2 + leaf_dev // 4
    capacity = leaf_dev * far_owner.shape[1] * 3 // 4
    me = lax.axis_index("leaf")
    core = lax.axis_index("rhs")
    swap = [(0, 1), (1, 0)]
    vmem = pl.BlockSpec(memory_space=pltpu.VMEM)
    smem = pl.BlockSpec(memory_space=pltpu.SMEM)
    params = pltpu.CompilerParams(vmem_limit_bytes=40 * 2**20)

    point_live = lax.broadcasted_iota(jnp.int32, (leaf_dev, leaf_size), 1) < counts[:, None]
    masked = jnp.where(point_live[:, None, :], values, jnp.zeros_like(values))
    table = pl.pallas_call(
        coef_kernel,
        out_shape=jax.ShapeDtypeStruct((pairs, 2 * DIM, 2 * rank), BF16),
        in_specs=[vmem] * 5,
        out_specs=vmem,
        compiler_params=params,
        cost_estimate=pl.CostEstimate(flops=10**8, bytes_accessed=6 * 2**20, transcendentals=0),
        name="coef",
    )(masked, leaf_basis, transfer, leaf_skeleton, upper_skeleton)
    gathered = plane_gather(table)
    skels = line_shifts(table[:, :DIM], 2)
    lists = unit_lists(far_owner, far_local, upper_owner, upper_local, capacity)
    all_lists = [lists[me % SIDE]]
    for r in range(1, SIDE):
        all_lists.append(line_shift(lists[(me - r) % SIDE], 2, r))

    bundle = jnp.concatenate([points, masked], axis=1)
    extended = with_halo(bundle, (("leaf", 0),), HALO)
    own = extended[:, DIM:]
    cols = jnp.concatenate([own, lax.ppermute(own, "rhs", swap)], axis=1)
    first_leaf = me * leaf_dev - HALO
    chosen = lax.dynamic_slice_in_dim(near_list - first_leaf, core * half, half, axis=0)
    start = core * half + HALO
    early = half * 5 // 8

    def near_ids(rows, offset):
        return jnp.concatenate([rows.reshape(-1), (start + offset)[None]]).astype(jnp.int32)

    near_first = near_field(
        near_ids(chosen[:early], 0), extended[:, :DIM], cols, early, near_count
    )
    theirs_first = lax.ppermute(near_first[:, columns:], "rhs", swap)
    gathered, _ = lax.optimization_barrier((gathered, near_first))

    parts = pl.pallas_call(
        functools.partial(far_kernel, 32),
        out_shape=jax.ShapeDtypeStruct((SIDE, pairs, columns, 2 * rank), F32),
        in_specs=[smem] * 4 + [vmem] * 5,
        out_specs=vmem,
        scratch_shapes=[
            pltpu.VMEM((SIDE * (2 * pairs + 1), columns, rank), F32),
        ],
        compiler_params=params,
        cost_estimate=pl.CostEstimate(
            flops=3 * 10**10, bytes_accessed=10 * 2**20, transcendentals=0
        ),
        name="far",
    )(*all_lists, gathered, *skels)
    total = lax.psum_scatter(
        parts, "leaf", scatter_dimension=0, axis_index_groups=lines(2), tiled=True
    )[0]

    late_ids, _ = lax.optimization_barrier((near_ids(chosen[early:], early), parts))
    near_last = near_field(late_ids, extended[:, :DIM], cols, half - early, near_count)
    theirs_last = lax.ppermute(near_last[:, columns:], "rhs", swap)
    near_half = jnp.concatenate([near_first, near_last], axis=0)
    near_theirs = jnp.concatenate([theirs_first, theirs_last], axis=0)

    limits = jnp.concatenate([counts, core[None]]).astype(jnp.int32)
    return pl.pallas_call(
        final_kernel,
        out_shape=jax.ShapeDtypeStruct((leaf_dev, columns, leaf_size), F32),
        in_specs=[smem] + [vmem] * 5,
        out_specs=vmem,
        compiler_params=params,
        name="final",
    )(limits, transfer, leaf_basis, near_half, near_theirs, total)


def solution(mesh):
    return jax.shard_map(
        body,
        mesh=mesh,
        in_specs=(
            P("leaf", None, None),
            P("leaf", "rhs", None),
            P("leaf"),
            P("leaf", None, None),
            P("leaf", None, None),
            P("leaf", None, None),
            P("leaf", None, None),
            P("leaf", None),
            P("leaf", None),
            P("leaf", None),
            P("leaf", None),
            P("leaf", None),
        ),
        out_specs=P("leaf", "rhs", None),
        check_vma=False,
    )
```

```python
import functools
import math

import jax
import jax.numpy as jnp
from jax import lax
from jax.experimental import pallas as pl
from jax.experimental.pallas import tpu as pltpu
from jax.sharding import PartitionSpec as P

DIM = 8
HALO = 4


SQRT_THREE = 1.7320508075688772
LENGTH_SCALE = 1.5


RATE = SQRT_THREE / LENGTH_SCALE
RATE_TWO = RATE * math.log2(math.e)
BF16 = jnp.bfloat16
F32 = jnp.float32


def matern_of_square(square):
    square = jnp.maximum(square, 1e-30)
    radius = square * lax.rsqrt(square)
    return ((1.0 + RATE * radius) * jnp.exp2(-RATE_TWO * radius)).astype(BF16)


def norm_rows(coords):
    norm = jnp.sum(coords * coords, axis=0, keepdims=True)
    high = norm.astype(BF16).astype(F32)
    middle = (norm - high).astype(BF16).astype(F32)
    low = norm - high - middle
    row = lax.broadcasted_iota(jnp.int32, coords.shape, 0)
    return row, high, middle, low


def source_form(coords):
    row, high, middle, low = norm_rows(coords)
    tail = jnp.where(row == 0, high, jnp.where(row == 1, middle, jnp.where(row == 2, low, 1.0)))
    return jnp.concatenate([coords, jnp.where(row < 6, tail, 0.0)], axis=0)


def target_form(coords):
    row, high, middle, low = norm_rows(coords)
    tail = jnp.where(row == 3, high, jnp.where(row == 4, middle, jnp.where(row == 5, low, 1.0)))
    return jnp.concatenate([-2.0 * coords, jnp.where(row < 6, tail, 0.0)], axis=0)


def near_kernel(near, leaves, ids, pts, cols, out, rows, mine, even, odd):
    half = out.shape[0]
    size = pts.shape[2]
    base = ids[half * near]

    group = 8

    def stage(k, carry):
        forms = [source_form(pts[k * group + n].astype(F32)) for n in range(group)]
        turned = [form.T.astype(BF16) for form in forms]
        for n in range(group):
            rows[k * group + n] = turned[n]
        return carry

    lax.fori_loop(0, leaves // group, stage, 0)

    def stage_target(k, carry):
        forms = [target_form(pts[base + k * group + n].astype(F32)) for n in range(group)]
        for n in range(group):
            mine[k * group + n] = forms[n].astype(BF16)
        return carry

    lax.fori_loop(0, half // group, stage_target, 0)

    def values(i, j, store):
        square = jnp.dot(rows[ids[i * near + j]], mine[i], preferred_element_type=F32)
        store[size * j : size * (j + 1), :] = matern_of_square(square)

    def phase(current, previous, store, ready):
        total = jnp.zeros((cols.shape[1], size), F32)
        for j in range(near):
            values(current, j, store)
            total = total + jnp.dot(
                cols[ids[previous * near + j]],
                ready[size * j : size * (j + 1), :],
                preferred_element_type=F32,
            )
        out[previous] = total

    for j in range(near):
        values(0, j, even)

    def step(k, carry):
        phase(2 * k + 1, 2 * k, odd, even)
        phase(jnp.minimum(2 * k + 2, half - 1), 2 * k + 1, even, odd)
        return carry

    lax.fori_loop(0, half // 2, step, 0)


def near_field(ids, pts, cols, half, near):
    leaves, _, size = pts.shape
    vmem = pl.BlockSpec(memory_space=pltpu.VMEM)
    return pl.pallas_call(
        functools.partial(near_kernel, near, leaves),
        out_shape=jax.ShapeDtypeStruct((half, cols.shape[1], size), F32),
        in_specs=[pl.BlockSpec(memory_space=pltpu.SMEM), vmem, vmem],
        out_specs=vmem,
        scratch_shapes=[
            pltpu.VMEM((leaves, size, 2 * DIM), BF16),
            pltpu.VMEM((half, 2 * DIM, size), BF16),
            pltpu.VMEM((near * size, size), BF16),
            pltpu.VMEM((near * size, size), BF16),
        ],
        compiler_params=pltpu.CompilerParams(vmem_limit_bytes=40 * 2**20),
        cost_estimate=pl.CostEstimate(
            flops=half * near * size * size * 64, bytes_accessed=4 * 2**20, transcendentals=0
        ),
        name="near",
    )(ids, pts, cols)


def with_halo(cells, sides, width):
    for axis, dim in sides:
        count = lax.axis_size(axis)
        ends = count - 1
        head = lax.slice_in_dim(cells, 0, width, axis=dim)
        tail = lax.slice_in_dim(cells, cells.shape[dim] - width, cells.shape[dim], axis=dim)
        cells = jnp.concatenate(
            [
                lax.ppermute(tail, axis, [(i, (i + 1) % count) for i in range(ends)]),
                cells,
                lax.ppermute(head, axis, [((i + 1) % count, i) for i in range(ends)]),
            ],
            axis=dim,
        )
    return cells


SIDE = 4


def coef_kernel(values, basis, transfer, leaf_skel, upper_skel, table):
    pairs = leaf_skel.shape[0] // 2
    step_pairs = 8

    def step(i, carry):
        first = i * step_pairs
        coefs = [
            lax.dot_general(
                values[2 * first + n],
                basis[2 * first + n],
                (((1,), (1,)), ((), ())),
                preferred_element_type=F32,
            )
            for n in range(2 * step_pairs)
        ]
        coefs = [jnp.concatenate(coefs[2 * n : 2 * n + 2], axis=1) for n in range(step_pairs)]
        upper = []
        for n in range(step_pairs):
            p = first + n
            stacked = jnp.concatenate([transfer[2 * p], transfer[2 * p + 1]], axis=0)
            upper.append(jnp.dot(coefs[n].astype(BF16), stacked, preferred_element_type=F32))
        for n in range(step_pairs):
            p = first + n
            skel = [leaf_skel[2 * p + k].astype(F32) for k in range(2)]
            table[p] = jnp.concatenate(
                [jnp.concatenate(skel, axis=1), coefs[n]], axis=0
            ).astype(BF16)
        for n in range(step_pairs // 2):
            p = i * (step_pairs // 2) + n
            skel = [upper_skel[2 * p + k].astype(F32) for k in range(2)]
            coef = jnp.concatenate(upper[2 * n : 2 * n + 2], axis=1)
            table[pairs + p] = jnp.concatenate(
                [jnp.concatenate(skel, axis=1), coef], axis=0
            ).astype(BF16)
        return carry

    lax.fori_loop(0, pairs // step_pairs, step, 0)


def far_kernel(units, *refs):
    lists, table, skels = refs[:4], refs[4], refs[5:9]
    outs, *sums = refs[9:]
    targets = 2 * skels[0].shape[0]
    rank = skels[0].shape[2] // 2
    lane = lax.broadcasted_iota(jnp.int32, (DIM, 2 * rank), 1)
    low = lane < rank

    def clear(i, carry):
        for n in range(4):
            for one in sums:
                one[i * 4 + n] = jnp.zeros(one.shape[1:], F32)
        return carry

    lax.fori_loop(0, sums[0].shape[0] // 4, clear, 0)

    def turned(array):
        return jnp.concatenate([array[:, rank:], array[:, :rank]], axis=1)

    for r in range(SIDE):
        listed, skel, first = lists[r], skels[r], r * (targets + 1)

        def step(i, carry):
            where, squares, weights = [], [], []
            for quad in range(units // 4):
                left, right, coefs = [], [], []
                for n in range(4):
                    entry = listed[i * units + quad * 4 + n]
                    target = entry >> 12
                    row = (entry >> 1) & 2047
                    source = table[row].astype(F32)
                    swap = (entry & 1) != (n % 2)
                    source = jnp.where(swap, turned(source), source)
                    keep = low if n % 2 == 0 else jnp.logical_not(low)
                    form = jnp.where(
                        jnp.concatenate([keep, keep], axis=0), source_form(source[:DIM]), 0.0
                    )
                    coef = jnp.where(keep, source[DIM:], 0.0)
                    blank = jnp.zeros_like(form)
                    empty = jnp.zeros_like(coef)
                    wide = [form, blank] if n < 2 else [blank, form]
                    right.append(jnp.concatenate(wide, axis=1))
                    wide = [coef, empty] if n < 2 else [empty, coef]
                    coefs.append(jnp.concatenate(wide, axis=1))
                    pair = skel[jnp.minimum(target, targets - 1) >> 1].astype(F32)
                    pair = jnp.where((target & 1) == 1, turned(pair), pair)
                    left.append(target_form(pair))
                    where.append(first + target)
                left = jnp.concatenate(left, axis=0)[:, :rank].astype(BF16)
                right = jnp.concatenate(right, axis=0).astype(BF16)
                weights.append(jnp.concatenate(coefs, axis=0).astype(BF16))
                squares.append(
                    lax.dot_general(
                        left, right, (((0,), (0,)), ((), ())), preferred_element_type=F32
                    )
                )
            kernels = [matern_of_square(square) for square in squares]
            fields = [
                lax.dot_general(
                    weight, kernel, (((1,), (1,)), ((), ())), preferred_element_type=F32
                )
                for weight, kernel in zip(weights, kernels)
            ]
            for n in range(units):
                at = DIM * (n % 4)
                sums[n % len(sums)][where[n]] += fields[n // 4][at : at + DIM]
            return carry

        count = listed[listed.shape[0] - 128]
        origin = listed[listed.shape[0] - 127]
        lax.fori_loop(0, (count + units - 1) // units, step, 0)

        def pack(k, carry):
            for n in range(8):
                p = k * 8 + n
                spots = [first + 2 * p, first + 2 * p + 1]
                both = [(sums[0][q] + sums[1][q]) + (sums[2][q] + sums[3][q]) for q in spots]
                outs[origin, p] = jnp.concatenate(both, axis=1)
            return carry

        lax.fori_loop(0, targets // 16, pack, 0)


def final_kernel(counts, transfer, basis, near_mine, near_theirs, total, out):
    leaves = out.shape[0]
    half = leaves // 2
    rank = transfer.shape[1]
    core = counts[leaves]
    lane = lax.broadcasted_iota(jnp.int32, out.shape[1:], 1)
    group = 16

    def step(i, carry):
        first = i * group
        upper = [total[half + first // 4 + n].astype(BF16) for n in range(group // 4)]
        down = [
            lax.dot_general(
                upper[n // 4][:, (n // 2 % 2) * rank : (n // 2 % 2 + 1) * rank],
                transfer[first + n],
                (((1,), (1,)), ((), ())),
                preferred_element_type=F32,
            )
            for n in range(group)
        ]
        pairs = [total[first // 2 + n] for n in range(group // 2)]
        field = [
            (pairs[n // 2][:, (n % 2) * rank : (n % 2 + 1) * rank] + down[n]).astype(BF16)
            for n in range(group)
        ]
        result = [
            jnp.dot(field[n], basis[first + n], preferred_element_type=F32) for n in range(group)
        ]
        owner = first // half
        inner = first - owner * half
        for n in range(group):
            near = jnp.where(
                owner == core, near_mine[inner + n][: out.shape[1]], near_theirs[inner + n]
            )
            out[first + n] = jnp.where(lane < counts[first + n], result[n] + near, 0.0)
        return carry

    lax.fori_loop(0, leaves // group, step, 0)


def lines(axis):
    stride = (SIDE * SIDE, SIDE, 1)[axis]
    starts = [i for i in range(SIDE**3) if i // stride % SIDE == 0]
    return [[start + stride * k for k in range(SIDE)] for start in starts]


def plane_gather(block):
    groups = [[SIDE * k + z for k in range(SIDE * SIDE)] for z in range(SIDE)]
    return lax.all_gather(block, "leaf", axis_index_groups=groups, tiled=True)


def line_shift(block, axis, by):
    pairs = [
        (line[(k + by) % SIDE], line[k]) for line in lines(axis) for k in range(SIDE)
    ]
    return lax.ppermute(block, "leaf", pairs)


def line_shifts(block, axis):
    return [block] + [line_shift(block, axis, by) for by in range(1, SIDE)]


def list_kernel(codes, lists):
    count = codes.shape[1]
    capacity = lists.shape[1] - 128
    code = codes[0:1, :]
    row = lax.broadcasted_iota(jnp.int32, (8, count), 0)
    hits = jnp.where(row == code >> 20, 1.0, 0.0)
    code = jnp.broadcast_to(code & (2**20 - 1), (8, count))
    digits = [code & 127, (code >> 7) & 127, code >> 14]
    weights = [hits * digit.astype(F32) for digit in digits] + [hits]
    weights = jnp.concatenate(weights, axis=0).astype(BF16)
    chunk = 256
    ranks = jnp.zeros((8, count), F32)
    for n in range(count // chunk):
        before = lax.broadcasted_iota(jnp.int32, (chunk, count), 0) + n * chunk
        after = lax.broadcasted_iota(jnp.int32, (chunk, count), 1)
        ranks = ranks + jnp.dot(
            hits[:, n * chunk : (n + 1) * chunk].astype(BF16),
            jnp.where(before < after, 1.0, 0.0).astype(BF16),
            preferred_element_type=F32,
        )
    rank = jnp.sum(ranks * hits, axis=0, keepdims=True).astype(jnp.int32)
    parts = capacity // chunk
    for n in range(parts):
        place = lax.broadcasted_iota(jnp.int32, (chunk, count), 0) + n * chunk
        spot = jnp.where(place == rank, 1.0, 0.0).astype(BF16)
        found = lax.dot_general(
            weights, spot, (((1,), (1,)), ((), ())), preferred_element_type=F32
        ).astype(jnp.int32)
        joined = found[:8] + (found[8:16] << 7) + (found[16:24] << 14)
        dummy = codes[1:2, 0:chunk]
        lists[:, n * chunk : (n + 1) * chunk] = jnp.where(found[24:] == 0, dummy, joined)
    total = jnp.sum(hits, axis=1, keepdims=True).astype(jnp.int32)
    lane = lax.broadcasted_iota(jnp.int32, (8, 128), 1)
    lists[:, capacity:] = jnp.where(lane == 0, total, codes[2:3, 0:128])


def unit_lists(leaf_owner, leaf_local, upper_owner, upper_local, capacity):
    me = lax.axis_index("leaf")
    leaves = leaf_owner.shape[0]
    parents = upper_owner.shape[0]
    pairs = (leaves + parents) // 2

    def coded(owner, local, first_pair, first_target):
        row = owner // SIDE * pairs + first_pair + local // 2
        target = first_target + lax.broadcasted_iota(jnp.int32, owner.shape, 0)
        return (owner % SIDE << 20) | (target << 12) | (row << 1) | (local & 1)

    code = jnp.concatenate(
        [
            coded(leaf_owner, leaf_local, 0, 0),
            coded(upper_owner, upper_local, leaves // 2, leaves),
        ],
        axis=0,
    ).reshape(1, -1)
    kind = lax.broadcasted_iota(jnp.int32, (8, code.shape[1]), 0)
    dummy = (leaves + parents) << 12
    codes = jnp.where(kind == 0, code, jnp.where(kind == 1, dummy, me % SIDE))
    vmem = pl.BlockSpec(memory_space=pltpu.VMEM)
    return pl.pallas_call(
        list_kernel,
        out_shape=jax.ShapeDtypeStruct((8, capacity + 128), jnp.int32),
        in_specs=[vmem],
        out_specs=vmem,
        compiler_params=pltpu.CompilerParams(vmem_limit_bytes=40 * 2**20),
        cost_estimate=pl.CostEstimate(flops=10**8, bytes_accessed=10**5, transcendentals=0),
        name="lists",
    )(codes)


def body(
    points,
    values,
    counts,
    leaf_basis,
    transfer,
    leaf_skeleton,
    upper_skeleton,
    near_list,
    far_owner,
    far_local,
    upper_owner,
    upper_local,
):
    leaf_dev = points.shape[0]
    leaf_size = points.shape[2]
    columns = values.shape[1]
    rank = leaf_basis.shape[1]
    near_count = near_list.shape[1]
    half = leaf_dev // 2
    pairs = leaf_dev // 2 + leaf_dev // 4
    capacity = leaf_dev * far_owner.shape[1] * 3 // 4
    me = lax.axis_index("leaf")
    core = lax.axis_index("rhs")
    swap = [(0, 1), (1, 0)]
    vmem = pl.BlockSpec(memory_space=pltpu.VMEM)
    smem = pl.BlockSpec(memory_space=pltpu.SMEM)
    params = pltpu.CompilerParams(vmem_limit_bytes=40 * 2**20)

    point_live = lax.broadcasted_iota(jnp.int32, (leaf_dev, leaf_size), 1) < counts[:, None]
    masked = jnp.where(point_live[:, None, :], values, jnp.zeros_like(values))
    table = pl.pallas_call(
        coef_kernel,
        out_shape=jax.ShapeDtypeStruct((pairs, 2 * DIM, 2 * rank), BF16),
        in_specs=[vmem] * 5,
        out_specs=vmem,
        compiler_params=params,
        cost_estimate=pl.CostEstimate(flops=10**8, bytes_accessed=6 * 2**20, transcendentals=0),
        name="coef",
    )(masked, leaf_basis, transfer, leaf_skeleton, upper_skeleton)
    gathered = plane_gather(table)
    skels = line_shifts(table[:, :DIM], 2)
    lists = unit_lists(far_owner, far_local, upper_owner, upper_local, capacity)
    all_lists = [lists[me % SIDE]]
    for r in range(1, SIDE):
        all_lists.append(line_shift(lists[(me - r) % SIDE], 2, r))

    bundle = jnp.concatenate([points, masked], axis=1)
    extended = with_halo(bundle, (("leaf", 0),), HALO)
    own = extended[:, DIM:]
    cols = jnp.concatenate([own, lax.ppermute(own, "rhs", swap)], axis=1)
    first_leaf = me * leaf_dev - HALO
    chosen = lax.dynamic_slice_in_dim(near_list - first_leaf, core * half, half, axis=0)
    start = core * half + HALO
    early = half * 5 // 8

    def near_ids(rows, offset):
        return jnp.concatenate([rows.reshape(-1), (start + offset)[None]]).astype(jnp.int32)

    near_first = near_field(
        near_ids(chosen[:early], 0), extended[:, :DIM], cols, early, near_count
    )
    theirs_first = lax.ppermute(near_first[:, columns:], "rhs", swap)
    gathered, _ = lax.optimization_barrier((gathered, near_first))

    parts = pl.pallas_call(
        functools.partial(far_kernel, 64),
        out_shape=jax.ShapeDtypeStruct((SIDE, pairs, columns, 2 * rank), F32),
        in_specs=[smem] * 4 + [vmem] * 5,
        out_specs=vmem,
        scratch_shapes=[
            pltpu.VMEM((SIDE * (2 * pairs + 1), columns, rank), F32) for _ in range(4)
        ],
        compiler_params=params,
        cost_estimate=pl.CostEstimate(
            flops=3 * 10**10, bytes_accessed=10 * 2**20, transcendentals=0
        ),
        name="far",
    )(*all_lists, gathered, *skels)
    total = lax.psum_scatter(
        parts, "leaf", scatter_dimension=0, axis_index_groups=lines(2), tiled=True
    )[0]

    late_ids, _ = lax.optimization_barrier((near_ids(chosen[early:], early), parts))
    near_last = near_field(late_ids, extended[:, :DIM], cols, half - early, near_count)
    theirs_last = lax.ppermute(near_last[:, columns:], "rhs", swap)
    near_half = jnp.concatenate([near_first, near_last], axis=0)
    near_theirs = jnp.concatenate([theirs_first, theirs_last], axis=0)

    limits = jnp.concatenate([counts, core[None]]).astype(jnp.int32)
    return pl.pallas_call(
        final_kernel,
        out_shape=jax.ShapeDtypeStruct((leaf_dev, columns, leaf_size), F32),
        in_specs=[smem] + [vmem] * 5,
        out_specs=vmem,
        compiler_params=params,
        name="final",
    )(limits, transfer, leaf_basis, near_half, near_theirs, total)


def solution(mesh):
    return jax.shard_map(
        body,
        mesh=mesh,
        in_specs=(
            P("leaf", None, None),
            P("leaf", "rhs", None),
            P("leaf"),
            P("leaf", None, None),
            P("leaf", None, None),
            P("leaf", None, None),
            P("leaf", None, None),
            P("leaf", None),
            P("leaf", None),
            P("leaf", None),
            P("leaf", None),
            P("leaf", None),
        ),
        out_specs=P("leaf", "rhs", None),
        check_vma=False,
    )
```
